128 devices in a mesh: gx: 16 (over y, z), gy: 4 (over x_hi, core), gz: 2 (over x_lo).
Axes of the slice: x: 4 (x_hi: 2, x_lo: 2; x = x_hi * 2 + x_lo), y: 4, z: 4, core: 2. Of those that a mesh axis runs over, the one named last changes fastest.
Arguments:
- blocks: bfloat16 [4, 16, 128, 256, 256], P('gy', 'gx'), may hold values from -0.0625 to 0.0625
- block_rows: int32 [4, 16, 128], P('gy', 'gx'), may hold values from 0 to 63
- block_cols: int32 [4, 16, 128], P('gy', 'gx'), may hold values from 0 to 15
- probe_bits: int32 [65536, 256], P(('gy', 'gx'), 'gz'), may hold values from 0 to 1
- shift: float32 [65536], P(('gy', 'gx')), may hold values from 0 to 0.7
Outputs:
- forms: float32 [3, 256], P(None, 'gz')
- last_term: float32 [65536, 256], P(('gy', 'gx'), 'gz')
The draws below stay inside these ranges and needn't reach their ends.
All inputs are finite; a program needn't handle non-finite values.
Results may differ from the reference program's by a relative error of at most 0.02.
Values may be sent and summed in bfloat16 or wider, within the bound.
A program may use at most 128 MiB of HBM per device.

```python
import jax
import jax.numpy as jnp
from jax import lax

BS = 256
RB_DEV = 4
KT = 128
NB = 256
NV = 65536
PROBES = 256
TROWS = 64
TCOLS = 16
N_GX = 16
N_GY = 4


def draw_shift(key, part):
    positions = jnp.arange(NV, dtype=jnp.int32)
    group = TROWS * BS
    across = (positions % group).astype(jnp.float32) / group
    upward = (positions // group).astype(jnp.float32) / (NV // group)
    rough = jax.random.uniform(key, (NV,), jnp.float32, -0.1, 0.1)
    return (0.1 + 0.4 * across + 0.1 * upward + rough).astype(jnp.float32)


def touch_ends(values, key, smallest, top_value):
    spot = [jax.random.randint(jax.random.fold_in(key, axis), (), 0, length) for axis, length in enumerate(values.shape)]
    main_axis = values.shape.index(max(values.shape))
    beside = spot[:main_axis] + [(spot[main_axis] + 1) % values.shape[main_axis]] + spot[main_axis + 1:]
    return values.at[tuple(spot)].set(smallest).at[tuple(beside)].set(top_value)


def block_scale(stream_key, shape, split, least, high):
    def one(axis_at, blocks):
        heights = jax.random.uniform(jax.random.fold_in(jax.random.fold_in(stream_key, 6), axis_at), (blocks,), jnp.float32, least / len(split), high / len(split))
        return jnp.repeat(jnp.exp(heights), shape[axis_at] // blocks).reshape((-1,) + (1,) * (len(shape) - axis_at - 1))

    level = one(*split[0])
    for cut in split[1:]:
        level = level * one(*cut)
    return level


def bell_draw(key, dims, scale, most, cuts=(), kind=jnp.bfloat16):
    loudness = block_scale(key, dims, cuts, -0.22, 0.18) if cuts else 1.0
    entries = jax.random.normal(key, dims, jnp.float32) * scale * loudness
    return jnp.minimum(jnp.maximum(entries, -most), most).astype(kind)


def setup_inputs(seed: int = 0) -> dict:
    streams_of = jax.random.split(jax.random.key(seed), 6)
    return {
        "blocks": bell_draw(streams_of[0], (N_GY, N_GX, KT, BS, BS), (KT * BS // RB_DEV) ** -0.5, 0.0625, ((0, 4), (1, 16))),
        "block_rows": touch_ends(jax.random.randint(streams_of[1], (N_GY, N_GX, KT), 0, TROWS), jax.random.fold_in(streams_of[1], 1), 0, TROWS - 1).astype(jnp.int32),
        "block_cols": touch_ends(jax.random.randint(streams_of[2], (N_GY, N_GX, KT), 0, TCOLS), jax.random.fold_in(streams_of[2], 1), 0, TCOLS - 1).astype(jnp.int32),
        "probe_bits": touch_ends(jax.random.randint(streams_of[3], (NV, PROBES), 0, 2), jax.random.fold_in(streams_of[3], 1), 0, 1).astype(jnp.int32),
        "shift": draw_shift(jax.random.fold_in(streams_of[5], 71), 0),
    }


def apply_operator(blocks, block_rows, block_cols, shift, field):
    rounded = field.astype(jnp.bfloat16).reshape(NB, BS, PROBES)
    flat_blocks = blocks.reshape(N_GY * N_GX, KT, BS, BS)
    flat_rows = block_rows.reshape(N_GY * N_GX, KT)
    flat_cols = block_cols.reshape(N_GY * N_GX, KT)
    tile_ids = jnp.arange(N_GY * N_GX, dtype=jnp.int32)

    def one_tile(total, items):
        tile_blocks, rows_here, cols_here, tile = items
        row_group = (tile // N_GX).astype(jnp.int32)
        col_group = tile % N_GX
        global_cols = ((cols_here // RB_DEV) * TROWS + col_group * RB_DEV + cols_here % RB_DEV).astype(jnp.int32)
        picked = rounded[global_cols].astype(jnp.float32)
        product = jnp.einsum('kab,kbp->kap', tile_blocks.astype(jnp.float32), picked)
        partial_value = jnp.zeros((TROWS, BS, PROBES), jnp.float32).at[rows_here.astype(jnp.int32)].add(product)
        partial_value = lax.optimization_barrier(partial_value.astype(jnp.bfloat16)).astype(jnp.float32)
        return total.at[row_group].add(partial_value), None

    start = jnp.zeros((N_GY, TROWS, BS, PROBES), jnp.float32)
    total, _ = lax.scan(one_tile, start, (flat_blocks, flat_rows, flat_cols, tile_ids))
    return total.reshape(NV, PROBES) + shift[:, None] * field


def reference(blocks, block_rows, block_cols, probe_bits, shift):
    signs = (2 * probe_bits - 1).astype(jnp.float32)
    first = apply_operator(blocks, block_rows, block_cols, shift, signs)
    second = 2.0 * apply_operator(blocks, block_rows, block_cols, shift, first) - signs
    third = 2.0 * apply_operator(blocks, block_rows, block_cols, shift, second) - first
    forms = jnp.stack([jnp.sum(signs * first, axis=0), jnp.sum(signs * second, axis=0), jnp.sum(signs * third, axis=0)])
    return forms, third
```

```python
import jax
import jax.numpy as jnp
from jax import lax
from jax.experimental import pallas as pl
from jax.experimental.pallas import tpu as pltpu
from jax.sharding import PartitionSpec as P

BS = 256
KT = 128
TR = 64
TC = 16
NP = 128
PC = 4
HB = BS // 2
QB = BS // 4
LOC = PC * BS
F32 = jnp.float32
BF16 = jnp.bfloat16
UNROLL = 4

CHUNKS = ((2, 0), (2, 1), (1, 2), (1, 3), (1, 0), (1, 1),
          (2, 2), (2, 3), (3, 0), (3, 1), (3, 2), (3, 3))
FIRST = ((0, 4), (6, 4), (4, 2), (10, 2))
SECOND = ((0, 2), (3, 2), (2, 1), (5, 1))


def kernel(code, last, blocks_hbm, bits, shift_in, out_hbm, forms,
           blocks, s, w, land, t, z, shift, p, r1, q, qown, r2, fsum, fs, fr,
           load_sem, out_sem, psend, qsend, rs_recv, sib_send, part_send, fwd_send,
           sib_recv, fwd_recv, part_recv, fsend, frecv):
    gx, gy, gz = lax.axis_index("gx"), lax.axis_index("gy"), lax.axis_index("gz")
    y, zc = gx // 4, gx % 4
    sib = {"gx": gx, "gy": gy + 1 - 2 * (gy % 2), "gz": gz}
    partner_gy = (gy + 2) % 4
    part = {"gx": gx, "gy": partner_gy, "gz": gz}

    def at_y(d):
        return {"gx": (y + d) % 4 * 4 + zc, "gy": gy, "gz": gz}

    def at_z(d):
        return {"gx": y * 4 + (zc + d) % 4, "gy": gy, "gz": gz}

    def at_gy(d):
        return {"gx": gx, "gy": (gy + d) % 4, "gz": gz}

    load = pltpu.make_async_copy(blocks_hbm, blocks, load_sem)
    load.start()

    barrier = pltpu.get_barrier_semaphore()
    for d in (1, 2, 3):
        for there in (at_y, at_z, at_gy):
            pl.semaphore_signal(barrier, inc=1, device_id=there(d), device_id_type=pl.DeviceIdType.MESH)

    def remote(src, dst, send, recv, where):
        return pltpu.make_async_remote_copy(
            src_ref=src, dst_ref=dst, send_sem=send, recv_sem=recv,
            device_id=where, device_id_type=pl.DeviceIdType.MESH)

    def wait_for(ref, sem):
        pltpu.make_async_copy(ref, ref, sem).wait()

    signs = (2 * bits[...] - 1).astype(F32)
    z[...] = signs
    t[0] = signs
    t[1] = jnp.zeros((LOC, NP), F32)
    for b in range(PC):
        land[0, gy * PC + b] = signs[b * BS:(b + 1) * BS].astype(BF16)
    for c in range(LOC // NP):
        shift[c * NP:(c + 1) * NP] = jnp.broadcast_to(shift_in[c:c + 1], (NP, NP)).T
    fsum[...] = jnp.zeros_like(fsum)
    s[KT] = jnp.zeros((BS, NP), BF16)

    def share(par, b):
        mine = land.at[par, gy * PC + b]
        remote(mine, mine, part_send.at[par], part_recv.at[par, b], part).start()
        remote(mine, mine, sib_send.at[par], sib_recv.at[par], sib).start()

    def forward(par, b):
        got = land.at[par, partner_gy * PC + b]
        wait_for(got, part_recv.at[par, b])
        remote(got, got, fwd_send.at[par], fwd_recv.at[par], sib).start()

    pl.semaphore_wait(barrier, 9)
    for b in range(PC):
        share(0, b)
    for b in range(PC):
        forward(0, b)
    load.wait()

    def apply(a, _):
        par = lax.rem(a, 2)
        nxt = 1 - par
        four = land.at[par, pl.ds(0, PC)]
        for sem in (sib_recv, fwd_recv):
            wait_for(four, sem.at[par])
        for sem in (sib_send, part_send, fwd_send):
            wait_for(four, sem.at[par])
        w[...] = land[par]

        def block(k, carry):
            acc, prev = carry
            e = code[k]
            row = e // (KT * TC)
            keep = (row == prev).astype(F32)
            prod = jnp.dot(blocks[e % KT], w[e // KT % TC], preferred_element_type=F32)
            acc = acc * keep + prod
            s[k] = acc.astype(BF16)
            return acc, row

        def group(g, carry):
            for u in range(UNROLL):
                carry = block(g * UNROLL + u, carry)
            return carry

        lax.fori_loop(0, KT // UNROLL, group, (jnp.zeros((BS, NP), F32), jnp.int32(-1)))

        first_axis, second_axis = (at_y, at_z), (at_z, at_y)

        def row_of(h, b, d1, d2):
            dy, dz = (d1, d2) if h == 0 else (d2, d1)
            return last[((y + dy) % 4 * 4 + (zc + dz) % 4) * PC + b]

        def half(h):
            return slice(h * HB, (h + 1) * HB)

        def send(buf, land_in, h, b, table, m, sem, axis, stage):
            at, n = table[m]
            src = buf.at[h, b, pl.ds(at, n)]
            remote(src, land_in.at[par, h, b, pl.ds(at, n)], sem,
                   rs_recv.at[par, h, b, stage, m], axis(1 if m % 2 == 0 else 3)).start()

        def arrived(land_in, h, b, table, m, stage):
            at, n = table[m]
            wait_for(land_in.at[par, h, b, pl.ds(at, n)], rs_recv.at[par, h, b, stage, m])

        def step1(b):
            for h in (0, 1):
                for m in (0, 1, 2, 3):
                    at, n = FIRST[m]
                    for c in range(at, at + n):
                        p[h, b, c] = s[row_of(h, b, *CHUNKS[c]), half(h)]
                    if m < 2:
                        send(p, r1, h, b, FIRST, m, psend, first_axis[h], 0)

        def step2(b):
            for m in (0, 1):
                for h in (0, 1):
                    arrived(r1, h, b, FIRST, m, 0)
                    at, n = FIRST[m + 2]
                    came = FIRST[m][0]
                    for c in range(n):
                        p[h, b, at + c] = (p[h, b, at + c].astype(F32) + r1[par, h, b, came + c].astype(F32)).astype(BF16)
                    send(p, r1, h, b, FIRST, m + 2, psend, first_axis[h], 0)

        def step3(b):
            for h in (0, 1):
                for m in (2, 3):
                    arrived(r1, h, b, FIRST, m, 0)
                sums = {}
                for d in (2, 1, 3, 0):
                    up, down = (4 + d, 8 + d) if d < 2 else (d, 8 + d)
                    sums[d] = (s[row_of(h, b, 0, d), half(h)].astype(F32)
                               + r1[par, h, b, up].astype(F32) + r1[par, h, b, down].astype(F32))
                    if d == 2:
                        q[h, b, 0] = sums[2][:QB].astype(BF16)
                        q[h, b, 3] = sums[2][QB:].astype(BF16)
                    if d == 1:
                        q[h, b, 2] = sums[1][:QB].astype(BF16)
                        q[h, b, 1] = sums[1][QB:].astype(BF16)
                        send(q, r2, h, b, SECOND, 0, qsend, second_axis[h], 1)
                    if d == 3:
                        q[h, b, 4] = sums[3][:QB].astype(BF16)
                        q[h, b, 5] = sums[3][QB:].astype(BF16)
                        send(q, r2, h, b, SECOND, 1, qsend, second_axis[h], 1)
                    if d == 0:
                        qown[h, b] = sums[0]

        def step4(b):
            for m in (0, 1):
                for h in (0, 1):
                    arrived(r2, h, b, SECOND, m, 1)
                    at, came = SECOND[m + 2][0], SECOND[m][0]
                    q[h, b, at] = (q[h, b, at].astype(F32) + r2[par, h, b, came].astype(F32)).astype(BF16)
                    send(q, r2, h, b, SECOND, m + 2, qsend, second_axis[h], 1)

        factor = jnp.where(a == 0, 1.0, 2.0).astype(F32)

        def step5(b):
            for h in (0, 1):
                for m in (2, 3):
                    arrived(r2, h, b, SECOND, m, 1)
                for o, (x1, x2) in ((0, (2, 4)), (QB, (1, 5))):
                    m_w = qown[h, b, o:o + QB] + r2[par, h, b, x1].astype(F32) + r2[par, h, b, x2].astype(F32)
                    at = b * BS + h * HB + o
                    rows = slice(at, at + QB)
                    new = factor * (m_w + shift[rows] * t[par, rows]) - t[nxt, rows]
                    t[nxt, rows] = new
                    land[nxt, gy * PC + b, h * HB + o:h * HB + o + QB] = new.astype(BF16)
                    fsum[a] += jnp.sum((z[rows] * new).reshape(QB // 8, 8, NP), axis=0)

            @pl.when(a < 2)
            def _():
                share(nxt, b)

        def step6(b):
            @pl.when(a < 2)
            def _():
                forward(nxt, b)

        step1(0)
        for now in range(1, PC + 5):
            for lag, step in ((0, step1), (1, step2), (2, step3), (3, step4), (4, step5), (5, step6)):
                b = now - lag
                if 0 <= b < PC:
                    step(b)
        wait_for(p, psend)
        wait_for(q, qsend)
        return 0

    lax.fori_loop(0, 3, apply, 0)

    result = pltpu.make_async_copy(t.at[1], out_hbm, out_sem)
    result.start()
    fs[0] = jnp.zeros((8, NP), F32)
    for k in range(3):
        fs[0, k:k + 1] = jnp.sum(fsum[k], axis=0, keepdims=True)
    for stage, there in enumerate((at_gy, at_y, at_z)):
        copies = [remote(fs.at[stage], fr.at[stage, d - 1], fsend.at[stage, d - 1], frecv.at[stage, d - 1], there(d))
                  for d in (1, 2, 3)]
        for copy in copies:
            copy.start()
        for copy in copies:
            copy.wait()
        total = fs[stage] + fr[stage, 0] + fr[stage, 1] + fr[stage, 2]
        if stage < 2:
            fs[stage + 1] = total
        else:
            forms[...] = total
    result.wait()


def in_row_order(rows, cols):
    k = jnp.arange(KT, dtype=jnp.int32)
    key = rows * KT + k
    rank = jnp.sum((key[None, :] < key[:, None]).astype(jnp.int32), axis=1)
    code = (rows * TC + cols) * KT + k
    code = jnp.sum(jnp.where(rank[None, :] == k[:, None], code[None, :], 0), axis=1)
    row = jnp.arange(TR, dtype=jnp.int32)[:, None]
    upto = jnp.sum((rows[None, :] <= row).astype(jnp.int32), axis=1)
    count = jnp.sum((rows[None, :] == row).astype(jnp.int32), axis=1)
    return code, jnp.where(count > 0, upto - 1, KT)


def body(blocks, block_rows, block_cols, probe_bits, shift):
    code, last = in_row_order(block_rows[0, 0], block_cols[0, 0])
    dma = pltpu.SemaphoreType.DMA
    out, forms = pl.pallas_call(
        kernel,
        out_shape=(
            jax.ShapeDtypeStruct((LOC, NP), F32),
            jax.ShapeDtypeStruct((8, NP), F32),
        ),
        in_specs=[
            pl.BlockSpec(memory_space=pltpu.SMEM),
            pl.BlockSpec(memory_space=pltpu.SMEM),
            pl.BlockSpec(memory_space=pl.ANY),
            pl.BlockSpec(memory_space=pltpu.VMEM),
            pl.BlockSpec(memory_space=pltpu.VMEM),
        ],
        out_specs=(
            pl.BlockSpec(memory_space=pl.ANY),
            pl.BlockSpec(memory_space=pltpu.VMEM),
        ),
        scratch_shapes=[
            pltpu.VMEM((KT, BS, BS), BF16),
            pltpu.VMEM((KT + 1, BS, NP), BF16),
            pltpu.VMEM((TC, BS, NP), BF16),
            pltpu.VMEM((2, TC, BS, NP), BF16),
            pltpu.VMEM((2, LOC, NP), F32),
            pltpu.VMEM((LOC, NP), F32),
            pltpu.VMEM((LOC, NP), F32),
            pltpu.VMEM((2, PC, 12, HB, NP), BF16),
            pltpu.VMEM((2, 2, PC, 12, HB, NP), BF16),
            pltpu.VMEM((2, PC, 6, QB, NP), BF16),
            pltpu.VMEM((2, PC, HB, NP), F32),
            pltpu.VMEM((2, 2, PC, 6, QB, NP), BF16),
            pltpu.VMEM((3, 8, NP), F32),
            pltpu.VMEM((3, 8, NP), F32),
            pltpu.VMEM((3, 3, 8, NP), F32),
            dma, dma, dma, dma,
            dma((2, 2, PC, 2, 4)),
            dma((2,)), dma((2,)), dma((2,)),
            dma((2,)), dma((2,)), dma((2, PC)),
            dma((3, 3)), dma((3, 3)),
        ],
        compiler_params=pltpu.CompilerParams(
            collective_id=0, has_side_effects=True, vmem_limit_bytes=58 * 2**20
        ),
        cost_estimate=pl.CostEstimate(
            flops=6 * KT * BS * BS * NP, bytes_accessed=18 * 2**20, transcendentals=0
        ),
    )(code, last, blocks[0, 0], probe_bits, shift.reshape(LOC // NP, NP))
    return forms[:3], out


def solution(mesh):
    return jax.shard_map(
        body,
        mesh=mesh,
        in_specs=(
            P("gy", "gx", None, None, None),
            P("gy", "gx", None),
            P("gy", "gx", None),
            P(("gy", "gx"), "gz"),
            P(("gy", "gx")),
        ),
        out_specs=(P(None, "gz"), P(("gy", "gx"), "gz")),
        check_vma=False,
    )
```

```python
import jax
import jax.numpy as jnp
from jax import lax
from jax.experimental import pallas as pl
from jax.experimental.pallas import tpu as pltpu
from jax.sharding import PartitionSpec as P

BS = 256
KT = 128
TR = 64
TC = 16
NP = 128
PC = 4
HB = BS // 2
QB = BS // 4
LOC = PC * BS
F32 = jnp.float32
BF16 = jnp.bfloat16
UNROLL = 32

CHUNKS = ((2, 0), (2, 1), (1, 2), (1, 3), (1, 0), (1, 1),
          (2, 2), (2, 3), (3, 0), (3, 1), (3, 2), (3, 3))
FIRST = ((0, 4), (6, 4), (4, 2), (10, 2))
SECOND = ((0, 2), (3, 2), (2, 1), (5, 1))


def kernel(code, last, blocks_hbm, bits, shift_in, out_hbm, forms,
           blocks, s, w, land, t, z, shift, p, r1, q, qown, r2, fsum, fs, fr,
           load_sem, out_sem, psend, qsend, rs_recv, sib_send, part_send, fwd_send,
           sib_recv, fwd_recv, part_recv, fsend, frecv):
    gx, gy, gz = lax.axis_index("gx"), lax.axis_index("gy"), lax.axis_index("gz")
    y, zc = gx // 4, gx % 4
    sib = {"gx": gx, "gy": gy + 1 - 2 * (gy % 2), "gz": gz}
    partner_gy = (gy + 2) % 4
    part = {"gx": gx, "gy": partner_gy, "gz": gz}

    def at_y(d):
        return {"gx": (y + d) % 4 * 4 + zc, "gy": gy, "gz": gz}

    def at_z(d):
        return {"gx": y * 4 + (zc + d) % 4, "gy": gy, "gz": gz}

    def at_gy(d):
        return {"gx": gx, "gy": (gy + d) % 4, "gz": gz}

    load = pltpu.make_async_copy(blocks_hbm, blocks, load_sem)
    load.start()

    barrier = pltpu.get_barrier_semaphore()
    for d in (1, 2, 3):
        for there in (at_y, at_z, at_gy):
            pl.semaphore_signal(barrier, inc=1, device_id=there(d), device_id_type=pl.DeviceIdType.MESH)

    def remote(src, dst, send, recv, where):
        return pltpu.make_async_remote_copy(
            src_ref=src, dst_ref=dst, send_sem=send, recv_sem=recv,
            device_id=where, device_id_type=pl.DeviceIdType.MESH)

    def wait_for(ref, sem):
        pltpu.make_async_copy(ref, ref, sem).wait()

    signs = (2 * bits[...] - 1).astype(F32)
    z[...] = signs
    t[0] = signs
    t[1] = jnp.zeros((LOC, NP), F32)
    for b in range(PC):
        land[0, gy * PC + b] = signs[b * BS:(b + 1) * BS].astype(BF16)
    for c in range(LOC // NP):
        shift[c * NP:(c + 1) * NP] = jnp.broadcast_to(shift_in[c:c + 1], (NP, NP)).T
    fsum[...] = jnp.zeros_like(fsum)
    s[KT] = jnp.zeros((BS, NP), BF16)

    def share(par, b):
        mine = land.at[par, gy * PC + b]
        remote(mine, mine, part_send.at[par], part_recv.at[par, b], part).start()
        remote(mine, mine, sib_send.at[par], sib_recv.at[par], sib).start()

    def forward(par, b):
        got = land.at[par, partner_gy * PC + b]
        wait_for(got, part_recv.at[par, b])
        remote(got, got, fwd_send.at[par], fwd_recv.at[par], sib).start()

    pl.semaphore_wait(barrier, 9)
    for b in range(PC):
        share(0, b)
    for b in range(PC):
        forward(0, b)
    load.wait()

    def apply(a, _):
        par = lax.rem(a, 2)
        nxt = 1 - par
        four = land.at[par, pl.ds(0, PC)]
        for sem in (sib_recv, fwd_recv):
            wait_for(four, sem.at[par])
        for sem in (sib_send, part_send, fwd_send):
            wait_for(four, sem.at[par])
        w[...] = land[par]

        def block(k, carry):
            acc, prev = carry
            e = code[k]
            row = e >> 11
            keep = (row == prev).astype(F32)
            prod = jnp.dot(blocks[e & 127], w[(e >> 7) & 15], preferred_element_type=F32)
            acc = acc * keep + prod
            s[k] = acc.astype(BF16)
            return acc, row

        def group(g, carry):
            for u in range(UNROLL):
                carry = block(g * UNROLL + u, carry)
            return carry

        lax.fori_loop(0, KT // UNROLL, group, (jnp.zeros((BS, NP), F32), jnp.int32(-1)))

        first_axis, second_axis = (at_y, at_z), (at_z, at_y)

        def row_of(h, b, d1, d2):
            dy, dz = (d1, d2) if h == 0 else (d2, d1)
            return last[((y + dy) % 4 * 4 + (zc + dz) % 4) * PC + b]

        def half(h):
            return slice(h * HB, (h + 1) * HB)

        def send(buf, land_in, h, b, table, m, sem, axis, stage):
            at, n = table[m]
            src = buf.at[h, b, pl.ds(at, n)]
            remote(src, land_in.at[par, h, b, pl.ds(at, n)], sem,
                   rs_recv.at[par, h, b, stage, m], axis(1 if m % 2 == 0 else 3)).start()

        def arrived(land_in, h, b, table, m, stage):
            at, n = table[m]
            wait_for(land_in.at[par, h, b, pl.ds(at, n)], rs_recv.at[par, h, b, stage, m])

        def step1(b):
            for h in (0, 1):
                for m in (0, 1, 2, 3):
                    at, n = FIRST[m]
                    for c in range(at, at + n):
                        p[h, b, c] = s[row_of(h, b, *CHUNKS[c]), half(h)]
                    if m < 2:
                        send(p, r1, h, b, FIRST, m, psend, first_axis[h], 0)

        def step2(b):
            for m in (0, 1):
                for h in (0, 1):
                    arrived(r1, h, b, FIRST, m, 0)
                    at, n = FIRST[m + 2]
                    came = FIRST[m][0]
                    for c in range(n):
                        p[h, b, at + c] = (p[h, b, at + c].astype(F32) + r1[par, h, b, came + c].astype(F32)).astype(BF16)
                    send(p, r1, h, b, FIRST, m + 2, psend, first_axis[h], 0)

        def step3(b):
            for h in (0, 1):
                for m in (2, 3):
                    arrived(r1, h, b, FIRST, m, 0)
                sums = {}
                for d in (2, 1, 3, 0):
                    up, down = (4 + d, 8 + d) if d < 2 else (d, 8 + d)
                    sums[d] = (s[row_of(h, b, 0, d), half(h)].astype(F32)
                               + r1[par, h, b, up].astype(F32) + r1[par, h, b, down].astype(F32))
                    if d == 2:
                        q[h, b, 0] = sums[2][:QB].astype(BF16)
                        q[h, b, 3] = sums[2][QB:].astype(BF16)
                    if d == 1:
                        q[h, b, 2] = sums[1][:QB].astype(BF16)
                        q[h, b, 1] = sums[1][QB:].astype(BF16)
                        send(q, r2, h, b, SECOND, 0, qsend, second_axis[h], 1)
                    if d == 3:
                        q[h, b, 4] = sums[3][:QB].astype(BF16)
                        q[h, b, 5] = sums[3][QB:].astype(BF16)
                        send(q, r2, h, b, SECOND, 1, qsend, second_axis[h], 1)
                    if d == 0:
                        qown[h, b] = sums[0]

        def step4(b):
            for m in (0, 1):
                for h in (0, 1):
                    arrived(r2, h, b, SECOND, m, 1)
                    at, came = SECOND[m + 2][0], SECOND[m][0]
                    q[h, b, at] = (q[h, b, at].astype(F32) + r2[par, h, b, came].astype(F32)).astype(BF16)
                    send(q, r2, h, b, SECOND, m + 2, qsend, second_axis[h], 1)

        factor = jnp.where(a == 0, 1.0, 2.0).astype(F32)

        def step5(b):
            for h in (0, 1):
                for m in (2, 3):
                    arrived(r2, h, b, SECOND, m, 1)
                for o, (x1, x2) in ((0, (2, 4)), (QB, (1, 5))):
                    m_w = qown[h, b, o:o + QB] + r2[par, h, b, x1].astype(F32) + r2[par, h, b, x2].astype(F32)
                    at = b * BS + h * HB + o
                    rows = slice(at, at + QB)
                    new = factor * (m_w + shift[rows] * t[par, rows]) - t[nxt, rows]
                    t[nxt, rows] = new
                    land[nxt, gy * PC + b, h * HB + o:h * HB + o + QB] = new.astype(BF16)
                    fsum[a] += jnp.sum((z[rows] * new).reshape(QB // 8, 8, NP), axis=0)

            @pl.when(a < 2)
            def _():
                share(nxt, b)

        def step6(b):
            @pl.when(a < 2)
            def _():
                forward(nxt, b)

        step1(0)
        for now in range(1, PC + 5):
            for lag, step in ((0, step1), (1, step2), (2, step3), (3, step4), (4, step5), (5, step6)):
                b = now - lag
                if 0 <= b < PC:
                    step(b)
        wait_for(p, psend)
        wait_for(q, qsend)
        return 0

    lax.fori_loop(0, 3, apply, 0)

    result = pltpu.make_async_copy(t.at[1], out_hbm, out_sem)
    result.start()
    fs[0] = jnp.zeros((8, NP), F32)
    for k in range(3):
        fs[0, k:k + 1] = jnp.sum(fsum[k], axis=0, keepdims=True)
    for stage, there in enumerate((at_gy, at_y, at_z)):
        copies = [remote(fs.at[stage], fr.at[stage, d - 1], fsend.at[stage, d - 1], frecv.at[stage, d - 1], there(d))
                  for d in (1, 2, 3)]
        for copy in copies:
            copy.start()
        for copy in copies:
            copy.wait()
        total = fs[stage] + fr[stage, 0] + fr[stage, 1] + fr[stage, 2]
        if stage < 2:
            fs[stage + 1] = total
        else:
            forms[...] = total[:3]
    result.wait()


def in_row_order(rows, cols):
    k = jnp.arange(KT, dtype=jnp.int32)
    key = rows * KT + k
    rank = jnp.sum((key[None, :] < key[:, None]).astype(jnp.int32), axis=1)
    code = (rows * TC + cols) * KT + k
    code = jnp.sum(jnp.where(rank[None, :] == k[:, None], code[None, :], 0), axis=1)
    row = jnp.arange(TR, dtype=jnp.int32)[:, None]
    upto = jnp.sum((rows[None, :] <= row).astype(jnp.int32), axis=1)
    count = jnp.sum((rows[None, :] == row).astype(jnp.int32), axis=1)
    return code, jnp.where(count > 0, upto - 1, KT)


def body(blocks, block_rows, block_cols, probe_bits, shift):
    code, last = in_row_order(block_rows[0, 0], block_cols[0, 0])
    dma = pltpu.SemaphoreType.DMA
    out, forms = pl.pallas_call(
        kernel,
        out_shape=(
            jax.ShapeDtypeStruct((LOC, NP), F32),
            jax.ShapeDtypeStruct((3, NP), F32),
        ),
        in_specs=[
            pl.BlockSpec(memory_space=pltpu.SMEM),
            pl.BlockSpec(memory_space=pltpu.SMEM),
            pl.BlockSpec(memory_space=pl.ANY),
            pl.BlockSpec(memory_space=pltpu.VMEM),
            pl.BlockSpec(memory_space=pltpu.VMEM),
        ],
        out_specs=(
            pl.BlockSpec(memory_space=pl.ANY),
            pl.BlockSpec(memory_space=pltpu.VMEM),
        ),
        scratch_shapes=[
            pltpu.VMEM((KT, BS, BS), BF16),
            pltpu.VMEM((KT + 1, BS, NP), BF16),
            pltpu.VMEM((TC, BS, NP), BF16),
            pltpu.VMEM((2, TC, BS, NP), BF16),
            pltpu.VMEM((2, LOC, NP), F32),
            pltpu.VMEM((LOC, NP), F32),
            pltpu.VMEM((LOC, NP), F32),
            pltpu.VMEM((2, PC, 12, HB, NP), BF16),
            pltpu.VMEM((2, 2, PC, 12, HB, NP), BF16),
            pltpu.VMEM((2, PC, 6, QB, NP), BF16),
            pltpu.VMEM((2, PC, HB, NP), F32),
            pltpu.VMEM((2, 2, PC, 6, QB, NP), BF16),
            pltpu.VMEM((3, 8, NP), F32),
            pltpu.VMEM((3, 8, NP), F32),
            pltpu.VMEM((3, 3, 8, NP), F32),
            dma, dma, dma, dma,
            dma((2, 2, PC, 2, 4)),
            dma((2,)), dma((2,)), dma((2,)),
            dma((2,)), dma((2,)), dma((2, PC)),
            dma((3, 3)), dma((3, 3)),
        ],
        compiler_params=pltpu.CompilerParams(
            collective_id=0, has_side_effects=True, vmem_limit_bytes=58 * 2**20
        ),
        cost_estimate=pl.CostEstimate(
            flops=6 * KT * BS * BS * NP, bytes_accessed=18 * 2**20, transcendentals=0
        ),
    )(code, last, blocks[0, 0], probe_bits, shift.reshape(LOC // NP, NP))
    return forms, out


def solution(mesh):
    return jax.shard_map(
        body,
        mesh=mesh,
        in_specs=(
            P("gy", "gx", None, None, None),
            P("gy", "gx", None),
            P("gy", "gx", None),
            P(("gy", "gx"), "gz"),
            P(("gy", "gx")),
        ),
        out_specs=(P(None, "gz"), P(("gy", "gx"), "gz")),
        check_vma=False,
    )
```

```python
import jax
import jax.numpy as jnp
from jax import lax
from jax.experimental import pallas as pl
from jax.experimental.pallas import tpu as pltpu
from jax.sharding import PartitionSpec as P

BS = 256
KT = 128
TR = 64
TC = 16
NP = 128
NC = 2
CP = NP // NC
HP = CP // 2
RB = 4
PC = 2
G = RB // PC
LOC = RB * BS
F32 = jnp.float32
BF16 = jnp.bfloat16
UNROLL = 32

CHUNKS = ((2, 0), (2, 1), (1, 2), (1, 3), (1, 0), (1, 1),
          (2, 2), (2, 3), (3, 0), (3, 1), (3, 2), (3, 3))
FIRST = ((0, 4), (6, 4), (4, 2), (10, 2))


def kernel(code, last, blocks_hbm, bits, shift, out_hbm, forms,
           blocks, s, w, land, t, z, p, r1, q, qown, r2, fsum, fs, fr, out,
           load_sem, out_sem, psend, qsend, rs1, rs2, sib_send, part_send, fwd_send,
           sib_recv, fwd_recv, part_recv, fsend, frecv):
    gx, gy, gz = lax.axis_index("gx"), lax.axis_index("gy"), lax.axis_index("gz")
    y, zc = gx // 4, gx % 4
    sib = {"gx": gx, "gy": gy + 1 - 2 * (gy % 2), "gz": gz}
    partner_gy = (gy + 2) % 4
    part = {"gx": gx, "gy": partner_gy, "gz": gz}

    def at_y(d):
        return {"gx": (y + d) % 4 * 4 + zc, "gy": gy, "gz": gz}

    def at_z(d):
        return {"gx": y * 4 + (zc + d) % 4, "gy": gy, "gz": gz}

    def at_gy(d):
        return {"gx": gx, "gy": (gy + d) % 4, "gz": gz}

    first_axis, second_axis = (at_y, at_z), (at_z, at_y)

    load = pltpu.make_async_copy(blocks_hbm, blocks, load_sem)
    load.start()

    barrier = pltpu.get_barrier_semaphore()
    for d in (1, 2, 3):
        for there in (at_y, at_z, at_gy):
            pl.semaphore_signal(barrier, inc=1, device_id=there(d), device_id_type=pl.DeviceIdType.MESH)

    def remote(src, dst, send, recv, where):
        return pltpu.make_async_remote_copy(
            src_ref=src, dst_ref=dst, send_sem=send, recv_sem=recv,
            device_id=where, device_id_type=pl.DeviceIdType.MESH)

    def wait_for(ref, sem):
        pltpu.make_async_copy(ref, ref, sem).wait()

    for r in range(LOC // NP):
        signs = (2 * bits[r * NP:(r + 1) * NP] - 1).astype(F32).T
        b, lanes = r // 2, slice(r % 2 * NP, r % 2 * NP + NP)
        for c in range(NC):
            for h in (0, 1):
                mine = signs[(2 * c + h) * HP:(2 * c + h + 1) * HP]
                z[c, h, b, :, lanes] = mine
                t[0, c, h, b, :, lanes] = mine
                land[c, 0, gy * RB + b, h * HP:(h + 1) * HP, lanes] = mine.astype(BF16)
    t[1] = jnp.zeros_like(t[1])
    fsum[...] = jnp.zeros_like(fsum)
    for c in range(NC):
        s[c, KT] = jnp.zeros((CP, BS), BF16)

    def share(c, par, g):
        mine = land.at[c, par, pl.ds(gy * RB + g * G, G)]
        remote(mine, mine, part_send.at[c, par], part_recv.at[c, par, g], part).start()
        remote(mine, mine, sib_send.at[c, par], sib_recv.at[c, par], sib).start()

    def forward(c, par, g):
        got = land.at[c, par, pl.ds(partner_gy * RB + g * G, G)]
        wait_for(got, part_recv.at[c, par, g])
        remote(got, got, fwd_send.at[c, par], fwd_recv.at[c, par], sib).start()

    def gathered(c, par):
        four = land.at[c, par, pl.ds(0, RB)]
        for sem in (sib_recv, fwd_recv, sib_send, part_send, fwd_send):
            wait_for(four, sem.at[c, par])

    def row_of(h, b, d1, d2):
        dy, dz = (d1, d2) if h == 0 else (d2, d1)
        return last[((y + dy) % 4 * 4 + (zc + dz) % 4) * RB + b]

    def partial(c, h, b, d1, d2):
        return s[c, row_of(h, b, d1, d2), h * HP:(h + 1) * HP]

    def fill(c, h, g, m):
        at, n = FIRST[m]
        for i in range(at, at + n):
            for k in range(G):
                p[c, h, g, i, k] = partial(c, h, g * G + k, *CHUNKS[i])

    def send1(c, par, h, g, m):
        at, n = FIRST[m]
        remote(p.at[c, h, g, pl.ds(at, n)], r1.at[c, par, h, g, pl.ds(at, n)], psend.at[c],
               rs1.at[c, par, h, g, m], first_axis[h](1 if m % 2 == 0 else 3)).start()

    def arrived1(c, par, h, g, m):
        at, n = FIRST[m]
        wait_for(r1.at[c, par, h, g, pl.ds(at, n)], rs1.at[c, par, h, g, m])

    def begin(c, par):
        for g in range(PC):
            for h in (0, 1):
                for m in (0, 1):
                    fill(c, h, g, m)
                    send1(c, par, h, g, m)
        for g in range(PC):
            for h in (0, 1):
                for m in (2, 3):
                    fill(c, h, g, m)

    def hand_on(c, par, g):
        for h in (0, 1):
            for m in (0, 1):
                arrived1(c, par, h, g, m)
                to, came = FIRST[m + 2][0], FIRST[m][0]
                for i in range(2):
                    p[c, h, g, to + i] = (p[c, h, g, to + i].astype(F32)
                                          + r1[c, par, h, g, came + i].astype(F32)).astype(BF16)
                send1(c, par, h, g, m + 2)

    def second(c, par, g):
        for h in (0, 1):
            for m in (2, 3):
                arrived1(c, par, h, g, m)
            for d in (2, 1, 3, 0):
                up, down = (4 + d, 8 + d) if d < 2 else (d, 8 + d)
                for k in range(G):
                    total = (partial(c, h, g * G + k, 0, d).astype(F32)
                             + r1[c, par, h, g, up, k].astype(F32) + r1[c, par, h, g, down, k].astype(F32))
                    if d:
                        q[c, h, g, d - 1, k] = total.astype(BF16)
                    else:
                        qown[c, h, g, k] = total
                if d:
                    remote(q.at[c, h, g, d - 1], r2.at[c, par, h, g, d - 1], qsend.at[c],
                           rs2.at[c, par, h, g, d - 1], second_axis[h](d)).start()

    def finish(c, a, par, g):
        nxt = 1 - par
        factor = jnp.where(a == 0, 1.0, 2.0).astype(F32)
        for h in (0, 1):
            for d in (0, 1, 2):
                wait_for(r2.at[c, par, h, g, d], rs2.at[c, par, h, g, d])
            for k in range(G):
                b = g * G + k
                m_w = qown[c, h, g, k]
                for d in (0, 1, 2):
                    m_w = m_w + r2[c, par, h, g, d, k].astype(F32)
                new = factor * (m_w + shift[b:b + 1] * t[par, c, h, b]) - t[nxt, c, h, b]
                t[nxt, c, h, b] = new
                land[c, nxt, gy * RB + b, h * HP:(h + 1) * HP] = new.astype(BF16)
                form = z[c, h, b] * new
                fsum[a, c, h] += form[:, :NP] + form[:, NP:]

        @pl.when(a < 2)
        def _():
            share(c, nxt, g)

    def pass_on(c, a, par, g):
        @pl.when(a < 2)
        def _():
            forward(c, 1 - par, g)

    def sent(c):
        wait_for(p.at[c], psend.at[c])
        wait_for(q.at[c], qsend.at[c])

    pl.semaphore_wait(barrier, 9)
    for c in range(NC):
        for g in range(PC):
            share(c, 0, g)
    for g in range(PC):
        forward(0, 0, g)
    load.wait()

    def phase(n, _):
        c, a = n % 2, n // 2
        par = a % 2
        o, a_o = 1 - c, (n + 1) // 2 - 1
        par_o = (n + 1) // 2 % 2
        par_o = 1 - par_o
        gathered(c, par)
        w[...] = land[c, par]

        def other(step, *more):
            @pl.when(n > 0)
            def _():
                step(*more)

        def block(k, carry):
            acc, prev = carry
            e = code[k]
            row = e >> 11
            keep = (row == prev).astype(F32)
            prod = lax.dot_general(w[(e >> 7) & 15], blocks[e & 127], (((1,), (1,)), ((), ())),
                                   preferred_element_type=F32)
            acc = acc * keep + prod
            s[c, k] = acc.astype(BF16)
            return acc, row

        def group(i, carry):
            for u in range(UNROLL):
                carry = block(i * UNROLL + u, carry)
            return carry

        carry = (jnp.zeros((CP, BS), F32), jnp.int32(-1))
        other(hand_on, o, par_o, 1)
        carry = group(0, carry)
        other(second, o, par_o, 0)

        @pl.when(n == 0)
        def _():
            for g in range(PC):
                forward(1, 0, g)

        carry = group(1, carry)
        other(second, o, par_o, 1)
        carry = group(2, carry)
        other(finish, o, a_o, par_o, 0)
        carry = group(3, carry)
        begin(c, par)
        other(finish, o, a_o, par_o, 1)
        other(pass_on, o, a_o, par_o, 0)
        hand_on(c, par, 0)
        other(pass_on, o, a_o, par_o, 1)
        other(sent, o)
        return 0

    lax.fori_loop(0, 3 * NC, phase, 0)
    hand_on(1, 0, 1)
    second(1, 0, 0)
    second(1, 0, 1)
    finish(1, 2, 0, 0)
    finish(1, 2, 0, 1)
    sent(1)

    for k in range(3):
        by_probe = fsum[k].reshape(NP, NP)
        fs[0, k:k + 1] = jnp.sum(by_probe.T, axis=0, keepdims=True)
    fs[0, 3:8] = jnp.zeros((5, NP), F32)
    for stage, there in enumerate((at_gy, at_y, at_z)):
        copies = [remote(fs.at[stage], fr.at[stage, d - 1], fsend.at[stage, d - 1], frecv.at[stage, d - 1], there(d))
                  for d in (1, 2, 3)]
        for copy in copies:
            copy.start()
        if stage == 0:
            for r in range(LOC // NP):
                part_rows = t[1, :, :, r // 2, :, r % 2 * NP:r % 2 * NP + NP].reshape(NP, NP)
                out[r * NP:(r + 1) * NP] = part_rows.T
            result = pltpu.make_async_copy(out, out_hbm, out_sem)
            result.start()
        for copy in copies:
            copy.wait()
        total = fs[stage] + fr[stage, 0] + fr[stage, 1] + fr[stage, 2]
        if stage < 2:
            fs[stage + 1] = total
        else:
            forms[...] = total[:3]
    result.wait()


def in_row_order(rows, cols):
    k = jnp.arange(KT, dtype=jnp.int32)
    key = rows * KT + k
    rank = jnp.sum((key[None, :] < key[:, None]).astype(jnp.int32), axis=1)
    code = (rows * TC + cols) * KT + k
    code = jnp.sum(jnp.where(rank[None, :] == k[:, None], code[None, :], 0), axis=1)
    row = jnp.arange(TR, dtype=jnp.int32)[:, None]
    upto = jnp.sum((rows[None, :] <= row).astype(jnp.int32), axis=1)
    count = jnp.sum((rows[None, :] == row).astype(jnp.int32), axis=1)
    return code, jnp.where(count > 0, upto - 1, KT)


def body(blocks, block_rows, block_cols, probe_bits, shift):
    code, last = in_row_order(block_rows[0, 0], block_cols[0, 0])
    dma = pltpu.SemaphoreType.DMA
    out, forms = pl.pallas_call(
        kernel,
        out_shape=(
            jax.ShapeDtypeStruct((LOC, NP), F32),
            jax.ShapeDtypeStruct((3, NP), F32),
        ),
        in_specs=[
            pl.BlockSpec(memory_space=pltpu.SMEM),
            pl.BlockSpec(memory_space=pltpu.SMEM),
            pl.BlockSpec(memory_space=pl.ANY),
            pl.BlockSpec(memory_space=pltpu.VMEM),
            pl.BlockSpec(memory_space=pltpu.VMEM),
        ],
        out_specs=(
            pl.BlockSpec(memory_space=pl.ANY),
            pl.BlockSpec(memory_space=pltpu.VMEM),
        ),
        scratch_shapes=[
            pltpu.VMEM((KT, BS, BS), BF16),
            pltpu.VMEM((NC, KT + 1, CP, BS), BF16),
            pltpu.VMEM((TC, CP, BS), BF16),
            pltpu.VMEM((NC, 2, TC, CP, BS), BF16),
            pltpu.VMEM((2, NC, 2, RB, HP, BS), F32),
            pltpu.VMEM((NC, 2, RB, HP, BS), F32),
            pltpu.VMEM((NC, 2, PC, 12, G, HP, BS), BF16),
            pltpu.VMEM((NC, 2, 2, PC, 12, G, HP, BS), BF16),
            pltpu.VMEM((NC, 2, PC, 3, G, HP, BS), BF16),
            pltpu.VMEM((NC, 2, PC, G, HP, BS), F32),
            pltpu.VMEM((NC, 2, 2, PC, 3, G, HP, BS), BF16),
            pltpu.VMEM((3, NC, 2, HP, NP), F32),
            pltpu.VMEM((3, 8, NP), F32),
            pltpu.VMEM((3, 3, 8, NP), F32),
            pltpu.VMEM((LOC, NP), F32),
            dma, dma,
            dma((NC,)), dma((NC,)),
            dma((NC, 2, 2, PC, 4)),
            dma((NC, 2, 2, PC, 3)),
            dma((NC, 2)), dma((NC, 2)), dma((NC, 2)),
            dma((NC, 2)), dma((NC, 2)), dma((NC, 2, PC)),
            dma((3, 3)), dma((3, 3)),
        ],
        compiler_params=pltpu.CompilerParams(
            collective_id=0, has_side_effects=True, vmem_limit_bytes=58 * 2**20
        ),
        cost_estimate=pl.CostEstimate(
            flops=6 * KT * BS * BS * NP, bytes_accessed=18 * 2**20, transcendentals=0
        ),
    )(code, last, blocks[0, 0], probe_bits, shift.reshape(RB, BS))
    return forms, out


def solution(mesh):
    return jax.shard_map(
        body,
        mesh=mesh,
        in_specs=(
            P("gy", "gx", None, None, None),
            P("gy", "gx", None),
            P("gy", "gx", None),
            P(("gy", "gx"), "gz"),
            P(("gy", "gx")),
        ),
        out_specs=(P(None, "gz"), P(("gy", "gx"), "gz")),
        check_vma=False,
    )
```

```python
import jax
import jax.numpy as jnp
from jax import lax
from jax.experimental import pallas as pl
from jax.experimental.pallas import tpu as pltpu
from jax.sharding import PartitionSpec as P

BS = 256
KT = 128
TR = 64
TC = 16
NP = 128
NC = 2
CP = NP // NC
HP = CP // 2
RB = 4
PC = 4
G = RB // PC
LOC = RB * BS
F32 = jnp.float32
BF16 = jnp.bfloat16
UNROLL = 32
UNROLL0 = 16
ORDER = ('h2', 'h3', 'm0', 'm1', 's0', 's1', 'm2', 's2', 's3', 'm3', 'b', 'f0', 'f1', 'f2', 'f3', 'H0', 'H1')
FIRST_ORDER = ('H0', 'H1')

CHUNKS = ((2, 0), (2, 1), (1, 2), (1, 3), (1, 0), (1, 1),
          (2, 2), (2, 3), (3, 0), (3, 1), (3, 2), (3, 3))
FIRST = ((0, 4), (6, 4), (4, 2), (10, 2))


def kernel(rows, cols, blocks_hbm, bits, shift, out_hbm, forms,
           blocks, sorted_blocks, s, w, land, t, z, p, own, r1, q, qown, r2, fsum, fs, fr, out,
           order_vmem, order, load_sem, order_sem, out_sem, psend, qsend, rs1, rs2, share_send, share_recv,
           fsend, frecv):
    gx, gy, gz = lax.axis_index("gx"), lax.axis_index("gy"), lax.axis_index("gz")
    y, zc = gx // 4, gx % 4
    def at_y(d):
        return {"gx": (y + d) % 4 * 4 + zc, "gy": gy, "gz": gz}

    def at_z(d):
        return {"gx": y * 4 + (zc + d) % 4, "gy": gy, "gz": gz}

    def at_gy(d):
        other_core = gy + 1 - 2 * (gy % 2)
        return {"gx": gx, "gy": ((gy if d == 2 else other_core) + (2 if d > 1 else 0)) % 4, "gz": gz}

    first_axis, second_axis = (at_y, at_z), (at_z, at_y)

    load = pltpu.make_async_copy(blocks_hbm, blocks, load_sem)
    load.start()

    barrier = pltpu.get_barrier_semaphore()
    for d in (1, 2, 3):
        for there in (at_y, at_z, at_gy):
            pl.semaphore_signal(barrier, inc=1, device_id=there(d), device_id_type=pl.DeviceIdType.MESH)

    def remote(src, dst, send, recv, where):
        return pltpu.make_async_remote_copy(
            src_ref=src, dst_ref=dst, send_sem=send, recv_sem=recv,
            device_id=where, device_id_type=pl.DeviceIdType.MESH)

    def wait_for(ref, sem):
        pltpu.make_async_copy(ref, ref, sem).wait()

    for r in range(LOC // NP):
        signs = (2 * bits[r * NP:(r + 1) * NP] - 1).astype(F32).T
        b, lanes = r // 2, slice(r % 2 * NP, r % 2 * NP + NP)
        for c in range(NC):
            for h in (0, 1):
                mine = signs[(2 * c + h) * HP:(2 * c + h + 1) * HP]
                z[c, h, b, :, lanes] = mine
                t[0, c, h, b, :, lanes] = mine
                land[c, 0, gy * RB + b, h * HP:(h + 1) * HP, lanes] = mine.astype(BF16)
    t[1] = jnp.zeros_like(t[1])
    fsum[...] = jnp.zeros_like(fsum)
    s[KT] = jnp.zeros((CP, BS), BF16)

    lane = lax.broadcasted_iota(jnp.int32, (KT, KT), 1)
    stored = lax.broadcasted_iota(jnp.int32, (KT, KT), 0)
    rows_across = jnp.broadcast_to(rows[...], (KT, KT))
    rows_down = rows_across.astype(F32).T.astype(jnp.int32)
    cols_down = jnp.broadcast_to(cols[...], (KT, KT)).astype(F32).T.astype(jnp.int32)
    before = rows_across * KT + lane < rows_down * KT + stored
    rank = jnp.sum(before.astype(jnp.int32), axis=1, keepdims=True)
    entry = (rows_down * TC + cols_down) * KT + stored
    order_vmem[...] = jnp.zeros_like(order_vmem)
    order_vmem[0:1] = jnp.sum(jnp.where(rank == lane, entry, 0), axis=0, keepdims=True)
    upto = jnp.sum((rows_down <= lane).astype(jnp.int32), axis=0, keepdims=True)
    held = jnp.sum((rows_down == lane).astype(jnp.int32), axis=0, keepdims=True)
    order_vmem[1:2] = jnp.where(held > 0, upto - 1, KT)
    ordering = pltpu.make_async_copy(order_vmem, order, order_sem)
    ordering.start()

    def share(c, par, g):
        mine = land.at[c, par, pl.ds(gy * RB + g * G, G)]
        for d in (2, 1, 3):
            remote(mine, mine, share_send.at[c, par, d - 1], share_recv.at[c, par, d - 1], at_gy(d)).start()

    def gathered(c, par):
        four = land.at[c, par, pl.ds(0, RB)]
        for sem in (share_recv, share_send):
            for d in (1, 2, 3):
                wait_for(four, sem.at[c, par, d - 1])

    def row_of(h, b, d1, d2):
        dy, dz = (d1, d2) if h == 0 else (d2, d1)
        return order[1, ((y + dy) % 4 * 4 + (zc + dz) % 4) * RB + b]

    def partial(h, b, d1, d2):
        return s[row_of(h, b, d1, d2), h * HP:(h + 1) * HP]

    def fill(c, h, g, m):
        at, n = FIRST[m]
        for i in range(at, at + n):
            for k in range(G):
                p[c, h, g, i, k] = partial(h, g * G + k, *CHUNKS[i])

    def send1(c, par, h, g, m):
        at, n = FIRST[m]
        remote(p.at[c, h, g, pl.ds(at, n)], r1.at[c, par, h, g, pl.ds(at, n)], psend.at[c],
               rs1.at[c, par, h, g, m], first_axis[h](1 if m % 2 == 0 else 3)).start()

    def arrived1(c, par, h, g, m):
        at, n = FIRST[m]
        wait_for(r1.at[c, par, h, g, pl.ds(at, n)], rs1.at[c, par, h, g, m])

    def begin(c, par):
        for g in range(PC):
            for h in (0, 1):
                for m in (0, 1):
                    fill(c, h, g, m)
                    send1(c, par, h, g, m)
        for g in range(PC):
            for h in (0, 1):
                for m in (2, 3):
                    fill(c, h, g, m)
                for d in range(4):
                    for k in range(G):
                        own[c, h, g, d, k] = partial(h, g * G + k, 0, d)

    def hand_on(c, par, g):
        for h in (0, 1):
            for m in (0, 1):
                arrived1(c, par, h, g, m)
                to, came = FIRST[m + 2][0], FIRST[m][0]
                for i in range(2):
                    p[c, h, g, to + i] = (p[c, h, g, to + i].astype(F32)
                                          + r1[c, par, h, g, came + i].astype(F32)).astype(BF16)
                send1(c, par, h, g, m + 2)

    def second(c, par, g):
        for h in (0, 1):
            for m in (2, 3):
                arrived1(c, par, h, g, m)
            for d in (2, 1, 3, 0):
                up, down = (4 + d, 8 + d) if d < 2 else (d, 8 + d)
                for k in range(G):
                    total = (own[c, h, g, d, k].astype(F32)
                             + r1[c, par, h, g, up, k].astype(F32) + r1[c, par, h, g, down, k].astype(F32))
                    if d:
                        q[c, h, g, d - 1, k] = total.astype(BF16)
                    else:
                        qown[c, h, g, k] = total
                if d:
                    remote(q.at[c, h, g, d - 1], r2.at[c, par, h, g, d - 1], qsend.at[c],
                           rs2.at[c, par, h, g, d - 1], second_axis[h](d)).start()

    def finish(c, a, par, g):
        nxt = 1 - par
        factor = jnp.where(a == 0, 1.0, 2.0).astype(F32)
        for h in (0, 1):
            for d in (0, 1, 2):
                wait_for(r2.at[c, par, h, g, d], rs2.at[c, par, h, g, d])
            for k in range(G):
                b = g * G + k
                m_w = qown[c, h, g, k]
                for d in (0, 1, 2):
                    m_w = m_w + r2[c, par, h, g, d, k].astype(F32)
                new = factor * (m_w + shift[b:b + 1] * t[par, c, h, b]) - t[nxt, c, h, b]
                t[nxt, c, h, b] = new
                land[c, nxt, gy * RB + b, h * HP:(h + 1) * HP] = new.astype(BF16)
                form = z[c, h, b] * new
                fsum[a, c, h] += form[:, :NP] + form[:, NP:]

        @pl.when(a < 2)
        def _():
            share(c, nxt, g)

    def sent(c):
        wait_for(p.at[c], psend.at[c])
        wait_for(q.at[c], qsend.at[c])

    pl.semaphore_wait(barrier, 9)
    for c in range(NC):
        for g in range(PC):
            share(c, 0, g)
    ordering.wait()
    load.wait()

    steps = {
        "h": lambda c, a, par, g: hand_on(c, par, g),
        "s": lambda c, a, par, g: second(c, par, g),
        "f": finish,
    }

    def block(k, carry, first):
        acc, prev = carry
        e = order[0, k]
        row = e >> 11
        keep = (row == prev).astype(F32)
        if first:
            columns = blocks[e & 127].T
            sorted_blocks[k] = columns
        else:
            columns = sorted_blocks[k]
        acc = acc * keep + jnp.dot(w[(e >> 7) & 15], columns, preferred_element_type=F32)
        s[k] = acc.astype(BF16)
        return acc, row

    def group(i, carry, first=False):
        per = UNROLL0 if first else UNROLL
        for u in range(per):
            carry = block(i * per + u, carry, first)
        return carry

    start = (jnp.zeros((CP, BS), F32), jnp.int32(-1))
    gathered(0, 0)
    w[...] = land[0, 0]
    lax.fori_loop(0, KT // UNROLL0, lambda i, carry: group(i, carry, True), start)
    begin(0, 0)
    for token in FIRST_ORDER:
        steps[token[0].lower()](0, 0, 0, int(token[1:]))

    def phase(n, _):
        c, a = n % 2, n // 2
        par = a % 2
        o, a_o = 1 - c, (n - 1) // 2
        par_o = a_o % 2
        gathered(c, par)
        w[...] = land[c, par]
        carry = start
        for token in ORDER:
            what, g = token[0], int(token[1:] or 0)
            if what == "m":
                carry = group(g, carry)
            elif what == "b":
                begin(c, par)
            elif what in "HSF":
                steps[what.lower()](c, a, par, g)
            else:
                steps[what](o, a_o, par_o, g)
        sent(o)
        return 0

    lax.fori_loop(1, 3 * NC, phase, 0)
    for token in ORDER:
        if token[0] in "hsf":
            steps[token[0]](1, 2, 0, int(token[1:]))
    sent(1)

    for k in range(3):
        by_probe = fsum[k].reshape(NP, NP)
        fs[0, k:k + 1] = jnp.sum(by_probe.T, axis=0, keepdims=True)
    fs[0, 3:8] = jnp.zeros((5, NP), F32)
    for stage, there in enumerate((at_gy, at_y, at_z)):
        copies = [remote(fs.at[stage], fr.at[stage, d - 1], fsend.at[stage, d - 1], frecv.at[stage, d - 1], there(d))
                  for d in (1, 2, 3)]
        for copy in copies:
            copy.start()
        if stage == 0:
            for r in range(LOC // NP):
                part_rows = t[1, :, :, r // 2, :, r % 2 * NP:r % 2 * NP + NP].reshape(NP, NP)
                out[r * NP:(r + 1) * NP] = part_rows.T
            result = pltpu.make_async_copy(out, out_hbm, out_sem)
            result.start()
        for copy in copies:
            copy.wait()
        total = fs[stage] + fr[stage, 0] + fr[stage, 1] + fr[stage, 2]
        if stage < 2:
            fs[stage + 1] = total
        else:
            forms[...] = total[:3]
    result.wait()


def body(blocks, block_rows, block_cols, probe_bits, shift):
    dma = pltpu.SemaphoreType.DMA
    out, forms = pl.pallas_call(
        kernel,
        out_shape=(
            jax.ShapeDtypeStruct((LOC, NP), F32),
            jax.ShapeDtypeStruct((3, NP), F32),
        ),
        in_specs=[
            pl.BlockSpec(memory_space=pltpu.VMEM),
            pl.BlockSpec(memory_space=pltpu.VMEM),
            pl.BlockSpec(memory_space=pl.ANY),
            pl.BlockSpec(memory_space=pltpu.VMEM),
            pl.BlockSpec(memory_space=pltpu.VMEM),
        ],
        out_specs=(
            pl.BlockSpec(memory_space=pl.ANY),
            pl.BlockSpec(memory_space=pltpu.VMEM),
        ),
        scratch_shapes=[
            pltpu.VMEM((KT, BS, BS), BF16),
            pltpu.VMEM((KT, BS, BS), BF16),
            pltpu.VMEM((KT + 1, CP, BS), BF16),
            pltpu.VMEM((TC, CP, BS), BF16),
            pltpu.VMEM((NC, 2, TC, CP, BS), BF16),
            pltpu.VMEM((2, NC, 2, RB, HP, BS), F32),
            pltpu.VMEM((NC, 2, RB, HP, BS), F32),
            pltpu.VMEM((NC, 2, PC, 12, G, HP, BS), BF16),
            pltpu.VMEM((NC, 2, PC, 4, G, HP, BS), BF16),
            pltpu.VMEM((NC, 2, 2, PC, 12, G, HP, BS), BF16),
            pltpu.VMEM((NC, 2, PC, 3, G, HP, BS), BF16),
            pltpu.VMEM((NC, 2, PC, G, HP, BS), F32),
            pltpu.VMEM((NC, 2, 2, PC, 3, G, HP, BS), BF16),
            pltpu.VMEM((3, NC, 2, HP, NP), F32),
            pltpu.VMEM((3, 8, NP), F32),
            pltpu.VMEM((3, 3, 8, NP), F32),
            pltpu.VMEM((LOC, NP), F32),
            pltpu.VMEM((8, KT), jnp.int32),
            pltpu.SMEM((8, KT), jnp.int32),
            dma, dma, dma,
            dma((NC,)), dma((NC,)),
            dma((NC, 2, 2, PC, 4)),
            dma((NC, 2, 2, PC, 3)),
            dma((NC, 2, 3)), dma((NC, 2, 3)),
            dma((3, 3)), dma((3, 3)),
        ],
        compiler_params=pltpu.CompilerParams(
            collective_id=0, has_side_effects=True, vmem_limit_bytes=60 * 2**20
        ),
        cost_estimate=pl.CostEstimate(
            flops=6 * KT * BS * BS * NP, bytes_accessed=18 * 2**20, transcendentals=0
        ),
    )(block_rows[0], block_cols[0], blocks[0, 0], probe_bits, shift.reshape(RB, BS))
    return forms, out


def solution(mesh):
    return jax.shard_map(
        body,
        mesh=mesh,
        in_specs=(
            P("gy", "gx", None, None, None),
            P("gy", "gx", None),
            P("gy", "gx", None),
            P(("gy", "gx"), "gz"),
            P(("gy", "gx")),
        ),
        out_specs=(P(None, "gz"), P(("gy", "gx"), "gz")),
        check_vma=False,
    )
```

```python
import jax
import jax.numpy as jnp
from jax import lax
from jax.experimental import pallas as pl
from jax.experimental.pallas import tpu as pltpu
from jax.sharding import PartitionSpec as P

BS = 256
KT = 128
TR = 64
TC = 16
NP = 128
NC = 2
CP = NP // NC
HP = CP // 2
RB = 4
PC = 4
G = RB // PC
LOC = RB * BS
F32 = jnp.float32
BF16 = jnp.bfloat16
UNROLL = 32
LOAD = 16
ORDER = ('w.0', 'm0.0', 's0.1', 'm1.0', 's1.1', 'm2.0', 's2.1', 'm3.0', 's3.1', 'b.0', 'f0.1', 'f1.1', 'f2.1', 'f3.1', 'e.1', 'h0.0', 'h1.0', 'h2.0', 'h3.0')


CHUNKS = ((2, 0), (2, 1), (1, 2), (1, 3), (1, 0), (1, 1),
          (2, 2), (2, 3), (3, 0), (3, 1), (3, 2), (3, 3))
FIRST = ((0, 4), (6, 4), (4, 2), (10, 2))


def kernel(rows, cols, blocks_hbm, bits, shift, out_hbm, forms,
           blocks, s, w, land, t, z, p, own, r1, q, qown, r2, fsum, fs, fr, out,
           order_vmem, order, load_sem, order_sem, out_sem, psend, qsend, rs1, rs2, share_send, share_recv,
           fsend, frecv):
    gx, gy, gz = lax.axis_index("gx"), lax.axis_index("gy"), lax.axis_index("gz")
    y, zc = gx // 4, gx % 4
    def at_y(d):
        return {"gx": (y + d) % 4 * 4 + zc, "gy": gy, "gz": gz}

    def at_z(d):
        return {"gx": y * 4 + (zc + d) % 4, "gy": gy, "gz": gz}

    def at_gy(d):
        other_core = gy + 1 - 2 * (gy % 2)
        return {"gx": gx, "gy": ((gy if d == 2 else other_core) + (2 if d > 1 else 0)) % 4, "gz": gz}

    first_axis, second_axis = (at_y, at_z), (at_z, at_y)

    def load(i):
        part = pl.ds(i * LOAD, LOAD)
        return pltpu.make_async_copy(blocks_hbm.at[part], blocks.at[part], load_sem.at[i])

    for i in range(KT // LOAD):
        load(i).start()

    barrier = pltpu.get_barrier_semaphore()
    for d in (1, 2, 3):
        for there in (at_y, at_z, at_gy):
            pl.semaphore_signal(barrier, inc=1, device_id=there(d), device_id_type=pl.DeviceIdType.MESH)

    def remote(src, dst, send, recv, where):
        return pltpu.make_async_remote_copy(
            src_ref=src, dst_ref=dst, send_sem=send, recv_sem=recv,
            device_id=where, device_id_type=pl.DeviceIdType.MESH)

    def wait_for(ref, sem):
        pltpu.make_async_copy(ref, ref, sem).wait()

    for r in range(LOC // NP):
        signs = (2 * bits[r * NP:(r + 1) * NP] - 1).astype(F32).T
        b, lanes = r // 2, slice(r % 2 * NP, r % 2 * NP + NP)
        for c in range(NC):
            for h in (0, 1):
                mine = signs[(2 * c + h) * HP:(2 * c + h + 1) * HP]
                z[c, h, b, :, lanes] = mine
                t[0, c, h, b, :, lanes] = mine
                land[c, 0, gy * RB + b, h * HP:(h + 1) * HP, lanes] = mine.astype(BF16)
    t[1] = jnp.zeros_like(t[1])
    fsum[...] = jnp.zeros_like(fsum)
    s[KT] = jnp.zeros((CP, BS), BF16)

    lane = lax.broadcasted_iota(jnp.int32, (KT, KT), 1)
    stored = lax.broadcasted_iota(jnp.int32, (KT, KT), 0)
    rows_across = jnp.broadcast_to(rows[...], (KT, KT))
    rows_down = rows_across.astype(F32).T.astype(jnp.int32)
    cols_down = jnp.broadcast_to(cols[...], (KT, KT)).astype(F32).T.astype(jnp.int32)
    before = rows_across * KT + lane < rows_down * KT + stored
    rank = jnp.sum(before.astype(jnp.int32), axis=1, keepdims=True)
    entry = (rows_down * TC + cols_down) * KT + stored
    order_vmem[...] = jnp.zeros_like(order_vmem)
    order_vmem[0:1] = jnp.sum(jnp.where(rank == lane, entry, 0), axis=0, keepdims=True)
    upto = jnp.sum((rows_down <= lane).astype(jnp.int32), axis=0, keepdims=True)
    held = jnp.sum((rows_down == lane).astype(jnp.int32), axis=0, keepdims=True)
    order_vmem[1:2] = jnp.where(held > 0, upto - 1, KT)
    ordering = pltpu.make_async_copy(order_vmem, order, order_sem)
    ordering.start()

    def share(c, par, g):
        mine = land.at[c, par, pl.ds(gy * RB + g * G, G)]
        for d in (2, 1, 3):
            remote(mine, mine, share_send.at[c, par, d - 1], share_recv.at[c, par, d - 1], at_gy(d)).start()

    def gathered(c, par):
        four = land.at[c, par, pl.ds(0, RB)]
        for sem in (share_recv, share_send):
            for d in (1, 2, 3):
                wait_for(four, sem.at[c, par, d - 1])

    def row_of(h, b, d1, d2):
        dy, dz = (d1, d2) if h == 0 else (d2, d1)
        return order[1, ((y + dy) % 4 * 4 + (zc + dz) % 4) * RB + b]

    def partial(h, b, d1, d2):
        return s[row_of(h, b, d1, d2), h * HP:(h + 1) * HP]

    def fill(c, h, g, m):
        at, n = FIRST[m]
        for i in range(at, at + n):
            for k in range(G):
                p[c, h, g, i, k] = partial(h, g * G + k, *CHUNKS[i])

    def send1(c, par, h, g, m):
        at, n = FIRST[m]
        remote(p.at[c, h, g, pl.ds(at, n)], r1.at[c, par, h, g, pl.ds(at, n)], psend.at[c],
               rs1.at[c, par, h, g, m], first_axis[h](1 if m % 2 == 0 else 3)).start()

    def arrived1(c, par, h, g, m):
        at, n = FIRST[m]
        wait_for(r1.at[c, par, h, g, pl.ds(at, n)], rs1.at[c, par, h, g, m])

    def begin(c, par):
        for g in range(PC):
            for h in (0, 1):
                for m in (0, 1):
                    fill(c, h, g, m)
                    send1(c, par, h, g, m)
        for g in range(PC):
            for h in (0, 1):
                for m in (2, 3):
                    fill(c, h, g, m)
                for d in range(4):
                    for k in range(G):
                        own[c, h, g, d, k] = partial(h, g * G + k, 0, d)

    def hand_on(c, par, g):
        for h in (0, 1):
            for m in (0, 1):
                arrived1(c, par, h, g, m)
                to, came = FIRST[m + 2][0], FIRST[m][0]
                for i in range(2):
                    p[c, h, g, to + i] = (p[c, h, g, to + i].astype(F32)
                                          + r1[c, par, h, g, came + i].astype(F32)).astype(BF16)
                send1(c, par, h, g, m + 2)

    def second(c, par, g):
        for h in (0, 1):
            for m in (2, 3):
                arrived1(c, par, h, g, m)
            for d in (2, 1, 3, 0):
                up, down = (4 + d, 8 + d) if d < 2 else (d, 8 + d)
                for k in range(G):
                    total = (own[c, h, g, d, k].astype(F32)
                             + r1[c, par, h, g, up, k].astype(F32) + r1[c, par, h, g, down, k].astype(F32))
                    if d:
                        q[c, h, g, d - 1, k] = total.astype(BF16)
                    else:
                        qown[c, h, g, k] = total
                if d:
                    remote(q.at[c, h, g, d - 1], r2.at[c, par, h, g, d - 1], qsend.at[c],
                           rs2.at[c, par, h, g, d - 1], second_axis[h](d)).start()

    def finish(c, a, par, g):
        nxt = 1 - par
        factor = jnp.where(a == 0, 1.0, 2.0).astype(F32)
        for h in (0, 1):
            for d in (0, 1, 2):
                wait_for(r2.at[c, par, h, g, d], rs2.at[c, par, h, g, d])
            for k in range(G):
                b = g * G + k
                m_w = qown[c, h, g, k]
                for d in (0, 1, 2):
                    m_w = m_w + r2[c, par, h, g, d, k].astype(F32)
                new = factor * (m_w + shift[b:b + 1] * t[par, c, h, b]) - t[nxt, c, h, b]
                t[nxt, c, h, b] = new
                land[c, nxt, gy * RB + b, h * HP:(h + 1) * HP] = new.astype(BF16)
                form = z[c, h, b] * new
                fsum[a, c, h] += form[:, :NP] + form[:, NP:]

        @pl.when(a < 2)
        def _():
            share(c, nxt, g)

    def sent(c):
        wait_for(p.at[c], psend.at[c])
        wait_for(q.at[c], qsend.at[c])

    pl.semaphore_wait(barrier, 9)
    for c in range(NC):
        for g in range(PC):
            share(c, 0, g)
    ordering.wait()

    def turn(i, _):
        load(i).wait()
        for u in range(LOAD):
            blocks[i * LOAD + u] = blocks[i * LOAD + u].T
        return 0

    lax.fori_loop(0, KT // LOAD, turn, 0)

    def block(k, carry):
        acc, prev = carry
        e = order[0, k]
        row = e >> 11
        keep = (row == prev).astype(F32)
        acc = acc * keep + jnp.dot(w[(e >> 7) & 15], blocks[e & 127], preferred_element_type=F32)
        s[k] = acc.astype(BF16)
        return acc, row

    def group(i, carry):
        for u in range(UNROLL):
            carry = block(i * UNROLL + u, carry)
        return carry

    def take(c, par):
        gathered(c, par)
        w[...] = land[c, par]

    steps = {
        "w": lambda c, a, par, g: take(c, par),
        "b": lambda c, a, par, g: begin(c, par),
        "h": lambda c, a, par, g: hand_on(c, par, g),
        "s": lambda c, a, par, g: second(c, par, g),
        "f": finish,
        "e": lambda c, a, par, g: sent(c),
    }

    def do(token, n):
        step, lag = token.split(".")
        m = n - int(lag)
        steps[step[0]](m % NC, m // NC, m // NC % 2, int(step[1:] or 0))

    def phase(n, _):
        carry = (jnp.zeros((CP, BS), F32), jnp.int32(-1))
        for token in ORDER:
            lag = int(token.split(".")[1])
            if token[0] == "m":
                carry = group(int(token[1:-2]), carry)
            elif lag == 0:
                do(token, n)
            else:
                @pl.when(n >= lag)
                def _():
                    do(token, n)
        return 0

    phases = 3 * NC
    lax.fori_loop(0, phases, phase, 0)
    for n in range(phases, phases + NC):
        for token in ORDER:
            if n - int(token.split(".")[1]) < phases and token[0] != "m":
                do(token, n)

    for k in range(3):
        by_probe = fsum[k].reshape(NP, NP)
        fs[0, k:k + 1] = jnp.sum(by_probe.T, axis=0, keepdims=True)
    fs[0, 3:8] = jnp.zeros((5, NP), F32)
    for stage, there in enumerate((at_gy, at_y, at_z)):
        copies = [remote(fs.at[stage], fr.at[stage, d - 1], fsend.at[stage, d - 1], frecv.at[stage, d - 1], there(d))
                  for d in (1, 2, 3)]
        for copy in copies:
            copy.start()
        if stage == 0:
            for r in range(LOC // NP):
                part_rows = t[1, :, :, r // 2, :, r % 2 * NP:r % 2 * NP + NP].reshape(NP, NP)
                out[r * NP:(r + 1) * NP] = part_rows.T
            result = pltpu.make_async_copy(out, out_hbm, out_sem)
            result.start()
        for copy in copies:
            copy.wait()
        total = fs[stage] + fr[stage, 0] + fr[stage, 1] + fr[stage, 2]
        if stage < 2:
            fs[stage + 1] = total
        else:
            forms[...] = total[:3]
    result.wait()


def body(blocks, block_rows, block_cols, probe_bits, shift):
    dma = pltpu.SemaphoreType.DMA
    out, forms = pl.pallas_call(
        kernel,
        out_shape=(
            jax.ShapeDtypeStruct((LOC, NP), F32),
            jax.ShapeDtypeStruct((3, NP), F32),
        ),
        in_specs=[
            pl.BlockSpec(memory_space=pltpu.VMEM),
            pl.BlockSpec(memory_space=pltpu.VMEM),
            pl.BlockSpec(memory_space=pl.ANY),
            pl.BlockSpec(memory_space=pltpu.VMEM),
            pl.BlockSpec(memory_space=pltpu.VMEM),
        ],
        out_specs=(
            pl.BlockSpec(memory_space=pl.ANY),
            pl.BlockSpec(memory_space=pltpu.VMEM),
        ),
        scratch_shapes=[
            pltpu.VMEM((KT, BS, BS), BF16),
            pltpu.VMEM((KT + 1, CP, BS), BF16),
            pltpu.VMEM((TC, CP, BS), BF16),
            pltpu.VMEM((NC, 2, TC, CP, BS), BF16),
            pltpu.VMEM((2, NC, 2, RB, HP, BS), F32),
            pltpu.VMEM((NC, 2, RB, HP, BS), F32),
            pltpu.VMEM((NC, 2, PC, 12, G, HP, BS), BF16),
            pltpu.VMEM((NC, 2, PC, 4, G, HP, BS), BF16),
            pltpu.VMEM((NC, 2, 2, PC, 12, G, HP, BS), BF16),
            pltpu.VMEM((NC, 2, PC, 3, G, HP, BS), BF16),
            pltpu.VMEM((NC, 2, PC, G, HP, BS), F32),
            pltpu.VMEM((NC, 2, 2, PC, 3, G, HP, BS), BF16),
            pltpu.VMEM((3, NC, 2, HP, NP), F32),
            pltpu.VMEM((3, 8, NP), F32),
            pltpu.VMEM((3, 3, 8, NP), F32),
            pltpu.VMEM((LOC, NP), F32),
            pltpu.VMEM((8, KT), jnp.int32),
            pltpu.SMEM((8, KT), jnp.int32),
            dma((KT // LOAD,)), dma, dma,
            dma((NC,)), dma((NC,)),
            dma((NC, 2, 2, PC, 4)),
            dma((NC, 2, 2, PC, 3)),
            dma((NC, 2, 3)), dma((NC, 2, 3)),
            dma((3, 3)), dma((3, 3)),
        ],
        compiler_params=pltpu.CompilerParams(
            collective_id=0, has_side_effects=True, vmem_limit_bytes=60 * 2**20
        ),
        cost_estimate=pl.CostEstimate(
            flops=6 * KT * BS * BS * NP, bytes_accessed=18 * 2**20, transcendentals=0
        ),
    )(block_rows[0], block_cols[0], blocks[0, 0], probe_bits, shift.reshape(RB, BS))
    return forms, out


def solution(mesh):
    return jax.shard_map(
        body,
        mesh=mesh,
        in_specs=(
            P("gy", "gx", None, None, None),
            P("gy", "gx", None),
            P("gy", "gx", None),
            P(("gy", "gx"), "gz"),
            P(("gy", "gx")),
        ),
        out_specs=(P(None, "gz"), P(("gy", "gx"), "gz")),
        check_vma=False,
    )
```

```python
import jax
import jax.numpy as jnp
from jax import lax
from jax.experimental import pallas as pl
from jax.experimental.pallas import tpu as pltpu
from jax.sharding import PartitionSpec as P

BS = 256
KT = 128
TR = 64
TC = 16
NP = 128
NC = 2
CP = NP // NC
HP = CP // 2
RB = 4
PC = 4
G = RB // PC
LOC = RB * BS
F32 = jnp.float32
BF16 = jnp.bfloat16
UNROLL = 32
LOAD = 16
ORDER = ('w.0', 'm0.0', 's0.1', 'm1.0', 's1.1', 'm2.0', 's2.1', 'm3.0', 's3.1', 'b.0', 'f0.1', 'f1.1', 'f2.1', 'f3.1', 'e.1', 'h0.0', 'h1.0', 'h2.0', 'h3.0')


CHUNKS = ((2, 0), (2, 1), (1, 2), (1, 3), (1, 0), (1, 1),
          (2, 2), (2, 3), (3, 0), (3, 1), (3, 2), (3, 3))
FIRST = ((0, 4), (6, 4), (4, 2), (10, 2))


def kernel(rows, cols, blocks_hbm, bits, shift, out_hbm, forms,
           blocks, s, w, land, t, z, zb, zg, p, own, r1, q, qown, r2, fsum, fs, fr, out,
           order_vmem, order, load_sem, order_sem, out_sem, psend, qsend, zsend, zrecv, rs1, rs2, share_send, share_recv,
           fsend, frecv):
    gx, gy, gz = lax.axis_index("gx"), lax.axis_index("gy"), lax.axis_index("gz")
    y, zc = gx // 4, gx % 4
    def at_y(d):
        return {"gx": (y + d) % 4 * 4 + zc, "gy": gy, "gz": gz}

    def at_z(d):
        return {"gx": y * 4 + (zc + d) % 4, "gy": gy, "gz": gz}

    def at_gy(d):
        other_core = gy + 1 - 2 * (gy % 2)
        return {"gx": gx, "gy": ((gy if d == 2 else other_core) + (2 if d > 1 else 0)) % 4, "gz": gz}

    first_axis, second_axis = (at_y, at_z), (at_z, at_y)

    def load(i):
        part = pl.ds(i * LOAD, LOAD)
        return pltpu.make_async_copy(blocks_hbm.at[part], blocks.at[part], load_sem.at[i])

    for i in range(KT // LOAD):
        load(i).start()

    barrier = pltpu.get_barrier_semaphore()
    for d in (1, 2, 3):
        for there in (at_y, at_z, at_gy):
            pl.semaphore_signal(barrier, inc=1, device_id=there(d), device_id_type=pl.DeviceIdType.MESH)

    def remote(src, dst, send, recv, where):
        return pltpu.make_async_remote_copy(
            src_ref=src, dst_ref=dst, send_sem=send, recv_sem=recv,
            device_id=where, device_id_type=pl.DeviceIdType.MESH)

    def wait_for(ref, sem):
        pltpu.make_async_copy(ref, ref, sem).wait()

    for r in range(LOC // NP):
        signs = (2 * bits[r * NP:(r + 1) * NP] - 1).astype(F32).T
        b, lanes = r // 2, slice(r % 2 * NP, r % 2 * NP + NP)
        for c in range(NC):
            for h in (0, 1):
                mine = signs[(2 * c + h) * HP:(2 * c + h + 1) * HP]
                z[c, h, b, :, lanes] = mine
                zb[c, h, b, :, lanes] = mine.astype(BF16)
                t[0, c, h, b, :, lanes] = mine
                land[c, 0, gy * RB + b, h * HP:(h + 1) * HP, lanes] = mine.astype(BF16)
    t[1] = jnp.zeros_like(t[1])
    fsum[...] = jnp.zeros_like(fsum)
    s[KT] = jnp.zeros((CP, BS), BF16)

    lane = lax.broadcasted_iota(jnp.int32, (KT, KT), 1)
    stored = lax.broadcasted_iota(jnp.int32, (KT, KT), 0)
    rows_across = jnp.broadcast_to(rows[...], (KT, KT))
    rows_down = rows_across.astype(F32).T.astype(jnp.int32)
    cols_down = jnp.broadcast_to(cols[...], (KT, KT)).astype(F32).T.astype(jnp.int32)
    before = rows_across * KT + lane < rows_down * KT + stored
    rank = jnp.sum(before.astype(jnp.int32), axis=1, keepdims=True)
    entry = (rows_down * TC + cols_down) * KT + stored
    order_vmem[...] = jnp.zeros_like(order_vmem)
    order_vmem[0:1] = jnp.sum(jnp.where(rank == lane, entry, 0), axis=0, keepdims=True)
    upto = jnp.sum((rows_down <= lane).astype(jnp.int32), axis=0, keepdims=True)
    held = jnp.sum((rows_down == lane).astype(jnp.int32), axis=0, keepdims=True)
    order_vmem[1:2] = jnp.where(held > 0, upto - 1, KT)
    ordering = pltpu.make_async_copy(order_vmem, order, order_sem)
    ordering.start()

    def share(c, par, g):
        mine = land.at[c, par, pl.ds(gy * RB + g * G, G)]
        for d in (2, 1, 3):
            remote(mine, mine, share_send.at[c, par, d - 1], share_recv.at[c, par, d - 1], at_gy(d)).start()

    def gathered(c, par):
        four = land.at[c, par, pl.ds(0, RB)]
        for sem in (share_recv, share_send):
            for d in (1, 2, 3):
                wait_for(four, sem.at[c, par, d - 1])

    def row_of(h, b, d1, d2):
        dy, dz = (d1, d2) if h == 0 else (d2, d1)
        return order[1, ((y + dy) % 4 * 4 + (zc + dz) % 4) * RB + b]

    def partial(h, b, d1, d2):
        return s[row_of(h, b, d1, d2), h * HP:(h + 1) * HP]

    def fill(c, h, g, m):
        at, n = FIRST[m]
        for i in range(at, at + n):
            for k in range(G):
                p[c, h, g, i, k] = partial(h, g * G + k, *CHUNKS[i])

    def send1(c, par, h, g, m):
        at, n = FIRST[m]
        remote(p.at[c, h, g, pl.ds(at, n)], r1.at[c, par, h, g, pl.ds(at, n)], psend.at[c],
               rs1.at[c, par, h, g, m], first_axis[h](1 if m % 2 == 0 else 3)).start()

    def arrived1(c, par, h, g, m):
        at, n = FIRST[m]
        wait_for(r1.at[c, par, h, g, pl.ds(at, n)], rs1.at[c, par, h, g, m])

    def begin(c, par):
        for g in range(PC):
            for h in (0, 1):
                for m in (0, 1):
                    fill(c, h, g, m)
                    send1(c, par, h, g, m)
        for g in range(PC):
            for h in (0, 1):
                for m in (2, 3):
                    fill(c, h, g, m)
                for d in range(4):
                    for k in range(G):
                        own[c, h, g, d, k] = partial(h, g * G + k, 0, d)

    def hand_on(c, par, g):
        for h in (0, 1):
            for m in (0, 1):
                arrived1(c, par, h, g, m)
                to, came = FIRST[m + 2][0], FIRST[m][0]
                for i in range(2):
                    p[c, h, g, to + i] = (p[c, h, g, to + i].astype(F32)
                                          + r1[c, par, h, g, came + i].astype(F32)).astype(BF16)
                send1(c, par, h, g, m + 2)

    def scale(a):
        return jnp.where(a == 0, 1.0, 2.0).astype(F32)

    def second(c, a, par, g):
        for h in (0, 1):
            form = jnp.zeros((HP, BS), F32)
            for m in (2, 3):
                arrived1(c, par, h, g, m)
            for d in (2, 1, 3, 0):
                up, down = (4 + d, 8 + d) if d < 2 else (d, 8 + d)
                for k in range(G):
                    total = (own[c, h, g, d, k].astype(F32)
                             + r1[c, par, h, g, up, k].astype(F32) + r1[c, par, h, g, down, k].astype(F32))
                    b = g * G + k
                    if d:
                        q[c, h, g, d - 1, k] = total.astype(BF16)
                        form = form + zg[c, h, d - 1, b].astype(F32) * (scale(a) * total)
                    else:
                        qown[c, h, g, k] = total
                        form = form + z[c, h, b] * (scale(a) * (total + shift[b:b + 1] * t[par, c, h, b])
                                                    - t[1 - par, c, h, b])
                if d:
                    remote(q.at[c, h, g, d - 1], r2.at[c, par, h, g, d - 1], qsend.at[c],
                           rs2.at[c, par, h, g, d - 1], second_axis[h](d)).start()
            fsum[a, c, h] += form[:, :NP] + form[:, NP:]

    def finish(c, a, par, g):
        nxt = 1 - par
        for h in (0, 1):
            for d in (0, 1, 2):
                wait_for(r2.at[c, par, h, g, d], rs2.at[c, par, h, g, d])
            for k in range(G):
                b = g * G + k
                m_w = qown[c, h, g, k]
                for d in (0, 1, 2):
                    m_w = m_w + r2[c, par, h, g, d, k].astype(F32)
                new = scale(a) * (m_w + shift[b:b + 1] * t[par, c, h, b]) - t[nxt, c, h, b]
                t[nxt, c, h, b] = new
                land[c, nxt, gy * RB + b, h * HP:(h + 1) * HP] = new.astype(BF16)

        @pl.when(a < 2)
        def _():
            share(c, nxt, g)

    def sent(c):
        wait_for(p.at[c], psend.at[c])
        wait_for(q.at[c], qsend.at[c])

    pl.semaphore_wait(barrier, 9)
    for c in range(NC):
        for g in range(PC):
            share(c, 0, g)
    for d in (1, 3, 2):
        for c in range(NC):
            for h in (0, 1):
                remote(zb.at[c, h], zg.at[c, h, 3 - d], zsend, zrecv, second_axis[h](d)).start()
    ordering.wait()

    def turn(i, _):
        load(i).wait()
        for u in range(LOAD):
            blocks[i * LOAD + u] = blocks[i * LOAD + u].T
        return 0

    lax.fori_loop(0, KT // LOAD, turn, 0)

    def block(k, carry):
        acc, prev = carry
        e = order[0, k]
        row = e >> 11
        keep = (row == prev).astype(F32)
        acc = acc * keep + jnp.dot(w[(e >> 7) & 15], blocks[e & 127], preferred_element_type=F32)
        s[k] = acc.astype(BF16)
        return acc, row

    def group(i, carry):
        for u in range(UNROLL):
            carry = block(i * UNROLL + u, carry)
        return carry

    def take(c, par):
        gathered(c, par)
        w[...] = land[c, par]

    steps = {
        "w": lambda c, a, par, g: take(c, par),
        "b": lambda c, a, par, g: begin(c, par),
        "h": lambda c, a, par, g: hand_on(c, par, g),
        "s": second,
        "f": finish,
        "e": lambda c, a, par, g: sent(c),
    }

    def do(token, n):
        step, lag = token.split(".")
        m = n - int(lag)
        steps[step[0]](m % NC, m // NC, m // NC % 2, int(step[1:] or 0))

    def phase(n, _):
        @pl.when(n == 1)
        def _():
            wait_for(zg, zrecv)
            wait_for(zg, zsend)

        carry = (jnp.zeros((CP, BS), F32), jnp.int32(-1))
        for token in ORDER:
            lag = int(token.split(".")[1])
            if token[0] == "m":
                carry = group(int(token[1:-2]), carry)
            elif lag == 0:
                do(token, n)
            else:
                @pl.when(n >= lag)
                def _():
                    do(token, n)
        return 0

    phases = 3 * NC
    lax.fori_loop(0, phases, phase, 0)

    def exchange(stage):
        there = (at_gy, at_y, at_z)[stage]
        return [remote(fs.at[stage], fr.at[stage, d - 1], fsend.at[stage, d - 1], frecv.at[stage, d - 1], there(d))
                for d in (2, 1, 3)]

    def total_of(stage):
        for copy in exchange(stage):
            copy.wait()
        return fs[stage] + fr[stage, 0] + fr[stage, 1] + fr[stage, 2]

    def go(stage):
        for copy in exchange(stage):
            copy.start()

    final = NC - 1
    for g in range(PC):
        second(final, 2, 0, g)
    fs[0] = jnp.zeros((8, NP), F32)
    for k in range(3):
        fs[0, k:k + 1] = jnp.sum(fsum[k].reshape(NP, NP).T, axis=0, keepdims=True)
    go(0)
    finish(final, 2, 0, 0)
    finish(final, 2, 0, 1)
    fs[1] = total_of(0)
    go(1)
    for g in range(2, PC):
        finish(final, 2, 0, g)
    for r in range(LOC // NP):
        part_rows = t[1, :, :, r // 2, :, r % 2 * NP:r % 2 * NP + NP].reshape(NP, NP)
        out[r * NP:(r + 1) * NP] = part_rows.T
    result = pltpu.make_async_copy(out, out_hbm, out_sem)
    result.start()
    sent(final)
    fs[2] = total_of(1)
    go(2)
    forms[...] = total_of(2)[:3]
    result.wait()


def body(blocks, block_rows, block_cols, probe_bits, shift):
    dma = pltpu.SemaphoreType.DMA
    out, forms = pl.pallas_call(
        kernel,
        out_shape=(
            jax.ShapeDtypeStruct((LOC, NP), F32),
            jax.ShapeDtypeStruct((3, NP), F32),
        ),
        in_specs=[
            pl.BlockSpec(memory_space=pltpu.VMEM),
            pl.BlockSpec(memory_space=pltpu.VMEM),
            pl.BlockSpec(memory_space=pl.ANY),
            pl.BlockSpec(memory_space=pltpu.VMEM),
            pl.BlockSpec(memory_space=pltpu.VMEM),
        ],
        out_specs=(
            pl.BlockSpec(memory_space=pl.ANY),
            pl.BlockSpec(memory_space=pltpu.VMEM),
        ),
        scratch_shapes=[
            pltpu.VMEM((KT, BS, BS), BF16),
            pltpu.VMEM((KT + 1, CP, BS), BF16),
            pltpu.VMEM((TC, CP, BS), BF16),
            pltpu.VMEM((NC, 2, TC, CP, BS), BF16),
            pltpu.VMEM((2, NC, 2, RB, HP, BS), F32),
            pltpu.VMEM((NC, 2, RB, HP, BS), F32),
            pltpu.VMEM((NC, 2, RB, HP, BS), BF16),
            pltpu.VMEM((NC, 2, 3, RB, HP, BS), BF16),
            pltpu.VMEM((NC, 2, PC, 12, G, HP, BS), BF16),
            pltpu.VMEM((NC, 2, PC, 4, G, HP, BS), BF16),
            pltpu.VMEM((NC, 2, 2, PC, 12, G, HP, BS), BF16),
            pltpu.VMEM((NC, 2, PC, 3, G, HP, BS), BF16),
            pltpu.VMEM((NC, 2, PC, G, HP, BS), F32),
            pltpu.VMEM((NC, 2, 2, PC, 3, G, HP, BS), BF16),
            pltpu.VMEM((3, NC, 2, HP, NP), F32),
            pltpu.VMEM((3, 8, NP), F32),
            pltpu.VMEM((3, 3, 8, NP), F32),
            pltpu.VMEM((LOC, NP), F32),
            pltpu.VMEM((8, KT), jnp.int32),
            pltpu.SMEM((8, KT), jnp.int32),
            dma((KT // LOAD,)), dma, dma,
            dma((NC,)), dma((NC,)),
            dma, dma,
            dma((NC, 2, 2, PC, 4)),
            dma((NC, 2, 2, PC, 3)),
            dma((NC, 2, 3)), dma((NC, 2, 3)),
            dma((3, 3)), dma((3, 3)),
        ],
        compiler_params=pltpu.CompilerParams(
            collective_id=0, has_side_effects=True, vmem_limit_bytes=60 * 2**20
        ),
        cost_estimate=pl.CostEstimate(
            flops=6 * KT * BS * BS * NP, bytes_accessed=18 * 2**20, transcendentals=0
        ),
    )(block_rows[0], block_cols[0], blocks[0, 0], probe_bits, shift.reshape(RB, BS))
    return forms, out


def solution(mesh):
    return jax.shard_map(
        body,
        mesh=mesh,
        in_specs=(
            P("gy", "gx", None, None, None),
            P("gy", "gx", None),
            P("gy", "gx", None),
            P(("gy", "gx"), "gz"),
            P(("gy", "gx")),
        ),
        out_specs=(P(None, "gz"), P(("gy", "gx"), "gz")),
        check_vma=False,
    )
```

```python
import jax
import jax.numpy as jnp
from jax import lax
from jax.experimental import pallas as pl
from jax.experimental.pallas import tpu as pltpu
from jax.sharding import PartitionSpec as P

BS = 256
KT = 128
TR = 64
TC = 16
NP = 128
NC = 2
CP = NP // NC
HP = CP // 2
RB = 4
PC = 4
G = RB // PC
LOC = RB * BS
F32 = jnp.float32
BF16 = jnp.bfloat16
UNROLL = 32
LOAD = 16
ORDER = ('w.0', 'm0.0', 's0.1', 'm1.0', 's1.1', 'm2.0', 's2.1', 'm3.0', 's3.1', 'b.0', 'f0.1', 'f1.1', 'f2.1', 'f3.1', 'e.1', 'h0.0', 'h1.0', 'h2.0', 'h3.0')


CHUNKS = ((2, 0), (2, 1), (1, 2), (1, 3), (1, 0), (1, 1),
          (2, 2), (2, 3), (3, 0), (3, 1), (3, 2), (3, 3))
FIRST = ((0, 4), (6, 4), (4, 2), (10, 2))


def kernel(rows, cols, blocks_hbm, bits, shift, out_hbm, forms,
           blocks, s, w, land, t, z, zb, zg, p, own, r1, q, qown, r2, fsum, fs, fr, out,
           order_vmem, order, load_sem, order_sem, out_sem, psend, qsend, zsend, zrecv, rs1, rs2, share_send, share_recv,
           fsend, frecv):
    gx, gy, gz = lax.axis_index("gx"), lax.axis_index("gy"), lax.axis_index("gz")
    y, zc = gx // 4, gx % 4
    def at_y(d):
        return {"gx": (y + d) % 4 * 4 + zc, "gy": gy, "gz": gz}

    def at_z(d):
        return {"gx": y * 4 + (zc + d) % 4, "gy": gy, "gz": gz}

    def at_gy(d):
        other_core = gy + 1 - 2 * (gy % 2)
        return {"gx": gx, "gy": ((gy if d == 2 else other_core) + (2 if d > 1 else 0)) % 4, "gz": gz}

    first_axis, second_axis = (at_y, at_z), (at_z, at_y)

    def load(i):
        part = pl.ds(i * LOAD, LOAD)
        return pltpu.make_async_copy(blocks_hbm.at[part], blocks.at[part], load_sem.at[i])

    for i in range(KT // LOAD):
        load(i).start()

    barrier = pltpu.get_barrier_semaphore()
    for d in (1, 2, 3):
        for there in (at_y, at_z, at_gy):
            pl.semaphore_signal(barrier, inc=1, device_id=there(d), device_id_type=pl.DeviceIdType.MESH)

    def remote(src, dst, send, recv, where):
        return pltpu.make_async_remote_copy(
            src_ref=src, dst_ref=dst, send_sem=send, recv_sem=recv,
            device_id=where, device_id_type=pl.DeviceIdType.MESH)

    def wait_for(ref, sem):
        pltpu.make_async_copy(ref, ref, sem).wait()

    for r in range(LOC // NP):
        signs = (2 * bits[r * NP:(r + 1) * NP] - 1).astype(F32).T
        b, lanes = r // 2, slice(r % 2 * NP, r % 2 * NP + NP)
        for c in range(NC):
            for h in (0, 1):
                mine = signs[(2 * c + h) * HP:(2 * c + h + 1) * HP]
                z[c, h, b, :, lanes] = mine
                zb[c, h, b, :, lanes] = mine.astype(BF16)
                t[0, c, h, b, :, lanes] = mine
                land[c, 0, gy * RB + b, h * HP:(h + 1) * HP, lanes] = mine.astype(BF16)
    t[1] = jnp.zeros_like(t[1])
    fsum[...] = jnp.zeros_like(fsum)
    s[KT] = jnp.zeros((CP, BS), BF16)

    lane = lax.broadcasted_iota(jnp.int32, (KT, KT), 1)
    stored = lax.broadcasted_iota(jnp.int32, (KT, KT), 0)
    rows_across = jnp.broadcast_to(rows[...], (KT, KT))
    rows_down = rows_across.astype(F32).T.astype(jnp.int32)
    cols_down = jnp.broadcast_to(cols[...], (KT, KT)).astype(F32).T.astype(jnp.int32)
    before = rows_across * KT + lane < rows_down * KT + stored
    rank = jnp.sum(before.astype(jnp.int32), axis=1, keepdims=True)
    entry = (rows_down * TC + cols_down) * KT + stored
    order_vmem[...] = jnp.zeros_like(order_vmem)
    order_vmem[0:1] = jnp.sum(jnp.where(rank == lane, entry, 0), axis=0, keepdims=True)
    upto = jnp.sum((rows_down <= lane).astype(jnp.int32), axis=0, keepdims=True)
    held = jnp.sum((rows_down == lane).astype(jnp.int32), axis=0, keepdims=True)
    order_vmem[1:2] = jnp.where(held > 0, upto - 1, KT)
    ordering = pltpu.make_async_copy(order_vmem, order, order_sem)
    ordering.start()

    def share(c, par, g):
        mine = land.at[c, par, pl.ds(gy * RB + g * G, G)]
        for d in (2, 1, 3):
            remote(mine, mine, share_send.at[c, par, d - 1], share_recv.at[c, par, d - 1], at_gy(d)).start()

    def gathered(c, par):
        four = land.at[c, par, pl.ds(0, RB)]
        for sem in (share_recv, share_send):
            for d in (1, 2, 3):
                wait_for(four, sem.at[c, par, d - 1])

    def row_of(h, b, d1, d2):
        dy, dz = (d1, d2) if h == 0 else (d2, d1)
        return order[1, ((y + dy) % 4 * 4 + (zc + dz) % 4) * RB + b]

    def partial(h, b, d1, d2):
        return s[row_of(h, b, d1, d2), h * HP:(h + 1) * HP]

    def fill(c, h, g, m):
        at, n = FIRST[m]
        for i in range(at, at + n):
            for k in range(G):
                p[c, h, g, i, k] = partial(h, g * G + k, *CHUNKS[i])

    def send1(c, par, h, g, m):
        at, n = FIRST[m]
        remote(p.at[c, h, g, pl.ds(at, n)], r1.at[c, par, h, g, pl.ds(at, n)], psend.at[c],
               rs1.at[c, par, h, g, m], first_axis[h](1 if m % 2 == 0 else 3)).start()

    def arrived1(c, par, h, g, m):
        at, n = FIRST[m]
        wait_for(r1.at[c, par, h, g, pl.ds(at, n)], rs1.at[c, par, h, g, m])

    def begin(c, par):
        for g in range(PC):
            for h in (0, 1):
                for m in (0, 1):
                    fill(c, h, g, m)
                    send1(c, par, h, g, m)
        for g in range(PC):
            for h in (0, 1):
                for m in (2, 3):
                    fill(c, h, g, m)
                for d in range(4):
                    for k in range(G):
                        own[c, h, g, d, k] = partial(h, g * G + k, 0, d)

    def hand_on(c, par, g):
        for h in (0, 1):
            for m in (0, 1):
                arrived1(c, par, h, g, m)
                to, came = FIRST[m + 2][0], FIRST[m][0]
                for i in range(2):
                    p[c, h, g, to + i] = (p[c, h, g, to + i].astype(F32)
                                          + r1[c, par, h, g, came + i].astype(F32)).astype(BF16)
                send1(c, par, h, g, m + 2)

    def scale(a):
        return jnp.where(a == 0, 1.0, 2.0).astype(F32)

    def second(c, a, par, g):
        for h in (0, 1):
            form = jnp.zeros((HP, BS), F32)
            for m in (2, 3):
                arrived1(c, par, h, g, m)
            for d in (2, 1, 3, 0):
                up, down = (4 + d, 8 + d) if d < 2 else (d, 8 + d)
                for k in range(G):
                    total = (own[c, h, g, d, k].astype(F32)
                             + r1[c, par, h, g, up, k].astype(F32) + r1[c, par, h, g, down, k].astype(F32))
                    b = g * G + k
                    if d:
                        q[c, h, g, d - 1, k] = total.astype(BF16)
                        form = form + zg[c, h, d - 1, b].astype(F32) * (scale(a) * total)
                    else:
                        qown[c, h, g, k] = total
                        form = form + z[c, h, b] * (scale(a) * (total + shift[:, b * BS:(b + 1) * BS] * t[par, c, h, b])
                                                    - t[1 - par, c, h, b])
                if d:
                    remote(q.at[c, h, g, d - 1], r2.at[c, par, h, g, d - 1], qsend.at[c],
                           rs2.at[c, par, h, g, d - 1], second_axis[h](d)).start()
            fsum[a, c, h] += form[:, :NP] + form[:, NP:]

    def finish(c, a, par, g):
        nxt = 1 - par
        for h in (0, 1):
            for d in (0, 1, 2):
                wait_for(r2.at[c, par, h, g, d], rs2.at[c, par, h, g, d])
            for k in range(G):
                b = g * G + k
                m_w = qown[c, h, g, k]
                for d in (0, 1, 2):
                    m_w = m_w + r2[c, par, h, g, d, k].astype(F32)
                new = scale(a) * (m_w + shift[:, b * BS:(b + 1) * BS] * t[par, c, h, b]) - t[nxt, c, h, b]
                t[nxt, c, h, b] = new
                land[c, nxt, gy * RB + b, h * HP:(h + 1) * HP] = new.astype(BF16)

        @pl.when(a < 2)
        def _():
            share(c, nxt, g)

    def sent(c):
        wait_for(p.at[c], psend.at[c])
        wait_for(q.at[c], qsend.at[c])

    pl.semaphore_wait(barrier, 9)
    for c in range(NC):
        for g in range(PC):
            share(c, 0, g)
    for d in (1, 3, 2):
        for c in range(NC):
            for h in (0, 1):
                remote(zb.at[c, h], zg.at[c, h, 3 - d], zsend, zrecv, second_axis[h](d)).start()
    ordering.wait()

    def turn(i, _):
        load(i).wait()
        for u in range(LOAD):
            blocks[i * LOAD + u] = blocks[i * LOAD + u].T
        return 0

    lax.fori_loop(0, KT // LOAD, turn, 0)

    def block(k, carry):
        acc, prev = carry
        e = order[0, k]
        row = e >> 11
        keep = (row == prev).astype(F32)
        acc = acc * keep + jnp.dot(w[(e >> 7) & 15], blocks[e & 127], preferred_element_type=F32)
        s[k] = acc.astype(BF16)
        return acc, row

    def group(i, carry):
        for u in range(UNROLL):
            carry = block(i * UNROLL + u, carry)
        return carry

    def take(c, par):
        gathered(c, par)
        w[...] = land[c, par]

    steps = {
        "w": lambda c, a, par, g: take(c, par),
        "b": lambda c, a, par, g: begin(c, par),
        "h": lambda c, a, par, g: hand_on(c, par, g),
        "s": second,
        "f": finish,
        "e": lambda c, a, par, g: sent(c),
    }

    def do(token, n):
        step, lag = token.split(".")
        m = n - int(lag)
        steps[step[0]](m % NC, m // NC, m // NC % 2, int(step[1:] or 0))

    def phase(n, _):
        @pl.when(n == 1)
        def _():
            wait_for(zg, zrecv)
            wait_for(zg, zsend)

        carry = (jnp.zeros((CP, BS), F32), jnp.int32(-1))
        for token in ORDER:
            lag = int(token.split(".")[1])
            if token[0] == "m":
                carry = group(int(token[1:-2]), carry)
            elif lag == 0:
                do(token, n)
            else:
                @pl.when(n >= lag)
                def _():
                    do(token, n)
        return 0

    phases = 3 * NC
    lax.fori_loop(0, phases, phase, 0)

    def exchange(stage):
        there = (at_gy, at_y, at_z)[stage]
        return [remote(fs.at[stage], fr.at[stage, d - 1], fsend.at[stage, d - 1], frecv.at[stage, d - 1], there(d))
                for d in (2, 1, 3)]

    def total_of(stage):
        for copy in exchange(stage):
            copy.wait()
        return fs[stage] + fr[stage, 0] + fr[stage, 1] + fr[stage, 2]

    def go(stage):
        for copy in exchange(stage):
            copy.start()

    final = NC - 1
    for g in range(PC):
        second(final, 2, 0, g)
    fs[0] = jnp.zeros((8, NP), F32)
    for k in range(3):
        fs[0, k:k + 1] = jnp.sum(fsum[k].reshape(NP, NP).T, axis=0, keepdims=True)
    go(0)
    finish(final, 2, 0, 0)
    finish(final, 2, 0, 1)
    fs[1] = total_of(0)
    go(1)
    for g in range(2, PC):
        finish(final, 2, 0, g)
    for r in range(LOC // NP):
        part_rows = t[1, :, :, r // 2, :, r % 2 * NP:r % 2 * NP + NP].reshape(NP, NP)
        out[r * NP:(r + 1) * NP] = part_rows.T
    result = pltpu.make_async_copy(out, out_hbm, out_sem)
    result.start()
    sent(final)
    fs[2] = total_of(1)
    go(2)
    forms[...] = total_of(2)[:3]
    result.wait()


def body(blocks, block_rows, block_cols, probe_bits, shift):
    dma = pltpu.SemaphoreType.DMA
    out, forms = pl.pallas_call(
        kernel,
        out_shape=(
            jax.ShapeDtypeStruct((LOC, NP), F32),
            jax.ShapeDtypeStruct((3, NP), F32),
        ),
        in_specs=[
            pl.BlockSpec(memory_space=pltpu.VMEM),
            pl.BlockSpec(memory_space=pltpu.VMEM),
            pl.BlockSpec(memory_space=pl.ANY),
            pl.BlockSpec(memory_space=pltpu.VMEM),
            pl.BlockSpec(memory_space=pltpu.VMEM),
        ],
        out_specs=(
            pl.BlockSpec(memory_space=pl.ANY),
            pl.BlockSpec(memory_space=pltpu.VMEM),
        ),
        scratch_shapes=[
            pltpu.VMEM((KT, BS, BS), BF16),
            pltpu.VMEM((KT + 1, CP, BS), BF16),
            pltpu.VMEM((TC, CP, BS), BF16),
            pltpu.VMEM((NC, 2, TC, CP, BS), BF16),
            pltpu.VMEM((2, NC, 2, RB, HP, BS), F32),
            pltpu.VMEM((NC, 2, RB, HP, BS), F32),
            pltpu.VMEM((NC, 2, RB, HP, BS), BF16),
            pltpu.VMEM((NC, 2, 3, RB, HP, BS), BF16),
            pltpu.VMEM((NC, 2, PC, 12, G, HP, BS), BF16),
            pltpu.VMEM((NC, 2, PC, 4, G, HP, BS), BF16),
            pltpu.VMEM((NC, 2, 2, PC, 12, G, HP, BS), BF16),
            pltpu.VMEM((NC, 2, PC, 3, G, HP, BS), BF16),
            pltpu.VMEM((NC, 2, PC, G, HP, BS), F32),
            pltpu.VMEM((NC, 2, 2, PC, 3, G, HP, BS), BF16),
            pltpu.VMEM((3, NC, 2, HP, NP), F32),
            pltpu.VMEM((3, 8, NP), F32),
            pltpu.VMEM((3, 3, 8, NP), F32),
            pltpu.VMEM((LOC, NP), F32),
            pltpu.VMEM((8, KT), jnp.int32),
            pltpu.SMEM((8, KT), jnp.int32),
            dma((KT // LOAD,)), dma, dma,
            dma((NC,)), dma((NC,)),
            dma, dma,
            dma((NC, 2, 2, PC, 4)),
            dma((NC, 2, 2, PC, 3)),
            dma((NC, 2, 3)), dma((NC, 2, 3)),
            dma((3, 3)), dma((3, 3)),
        ],
        compiler_params=pltpu.CompilerParams(
            collective_id=0, has_side_effects=True, vmem_limit_bytes=60 * 2**20
        ),
        cost_estimate=pl.CostEstimate(
            flops=6 * KT * BS * BS * NP, bytes_accessed=18 * 2**20, transcendentals=0
        ),
    )(block_rows[0], block_cols[0], blocks[0, 0], probe_bits, shift[None])
    return forms, out


def solution(mesh):
    return jax.shard_map(
        body,
        mesh=mesh,
        in_specs=(
            P("gy", "gx", None, None, None),
            P("gy", "gx", None),
            P("gy", "gx", None),
            P(("gy", "gx"), "gz"),
            P(("gy", "gx")),
        ),
        out_specs=(P(None, "gz"), P(("gy", "gx"), "gz")),
        check_vma=False,
    )
```

```python
import jax
import jax.numpy as jnp
from jax import lax
from jax.experimental import pallas as pl
from jax.experimental.pallas import tpu as pltpu
from jax.sharding import PartitionSpec as P

BS = 256
KT = 128
TR = 64
TC = 16
NP = 128
NC = 2
CP = NP // NC
HP = CP // 2
RB = 4
PC = 4
G = RB // PC
LOC = RB * BS
F32 = jnp.float32
BF16 = jnp.bfloat16
UNROLL = 32
LOAD = 16
ORDER = ('w.0', 'm0.0', 's0.1', 'm1.0', 's1.1', 'm2.0', 's2.1', 'm3.0', 's3.1', 'b.0', 'f0.1', 'f1.1', 'f2.1', 'f3.1', 'e.1', 'h0.0', 'h1.0', 'h2.0', 'h3.0')


CHUNKS = ((2, 0), (2, 1), (1, 2), (1, 3), (1, 0), (1, 1),
          (2, 2), (2, 3), (3, 0), (3, 1), (3, 2), (3, 3))
FIRST = ((0, 2), (6, 2), (2, 2), (8, 2), (4, 2), (10, 2))


def kernel(rows, cols, blocks_hbm, bits, shift, out_hbm, forms,
           blocks, s, w, land, t, z, zb, zg, p, own, r1, q, qown, r2, fsum, fs, fr, out,
           order_vmem, order, load_sem, order_sem, out_sem, psend, qsend, zsend, zrecv, rs1, rs2, share_send, share_recv,
           fsend, frecv):
    gx, gy, gz = lax.axis_index("gx"), lax.axis_index("gy"), lax.axis_index("gz")
    y, zc = gx // 4, gx % 4
    def at_y(d):
        return {"gx": (y + d) % 4 * 4 + zc, "gy": gy, "gz": gz}

    def at_z(d):
        return {"gx": y * 4 + (zc + d) % 4, "gy": gy, "gz": gz}

    def at_gy(d):
        other_core = gy + 1 - 2 * (gy % 2)
        return {"gx": gx, "gy": ((gy if d == 2 else other_core) + (2 if d > 1 else 0)) % 4, "gz": gz}

    first_axis, second_axis = (at_y, at_z), (at_z, at_y)

    def load(i):
        part = pl.ds(i * LOAD, LOAD)
        return pltpu.make_async_copy(blocks_hbm.at[part], blocks.at[part], load_sem.at[i])

    for i in range(KT // LOAD):
        load(i).start()

    barrier = pltpu.get_barrier_semaphore()
    for d in (1, 2, 3):
        for there in (at_y, at_z, at_gy):
            pl.semaphore_signal(barrier, inc=1, device_id=there(d), device_id_type=pl.DeviceIdType.MESH)

    def remote(src, dst, send, recv, where):
        return pltpu.make_async_remote_copy(
            src_ref=src, dst_ref=dst, send_sem=send, recv_sem=recv,
            device_id=where, device_id_type=pl.DeviceIdType.MESH)

    def wait_for(ref, sem):
        pltpu.make_async_copy(ref, ref, sem).wait()

    for r in range(LOC // NP):
        signs = (2 * bits[r * NP:(r + 1) * NP] - 1).astype(F32).T
        b, lanes = r // 2, slice(r % 2 * NP, r % 2 * NP + NP)
        for c in range(NC):
            for h in (0, 1):
                mine = signs[(2 * c + h) * HP:(2 * c + h + 1) * HP]
                z[c, h, b, :, lanes] = mine
                zb[c, h, b, :, lanes] = mine.astype(BF16)
                t[0, c, h, b, :, lanes] = mine
                land[c, 0, gy * RB + b, h * HP:(h + 1) * HP, lanes] = mine.astype(BF16)
    t[1] = jnp.zeros_like(t[1])
    fsum[...] = jnp.zeros_like(fsum)
    s[KT] = jnp.zeros((CP, BS), BF16)

    lane = lax.broadcasted_iota(jnp.int32, (KT, KT), 1)
    stored = lax.broadcasted_iota(jnp.int32, (KT, KT), 0)
    rows_across = jnp.broadcast_to(rows[...], (KT, KT))
    rows_down = rows_across.astype(F32).T.astype(jnp.int32)
    cols_down = jnp.broadcast_to(cols[...], (KT, KT)).astype(F32).T.astype(jnp.int32)
    before = rows_across * KT + lane < rows_down * KT + stored
    rank = jnp.sum(before.astype(jnp.int32), axis=1, keepdims=True)
    entry = (rows_down * TC + cols_down) * KT + stored
    order_vmem[...] = jnp.zeros_like(order_vmem)
    order_vmem[0:1] = jnp.sum(jnp.where(rank == lane, entry, 0), axis=0, keepdims=True)
    upto = jnp.sum((rows_down <= lane).astype(jnp.int32), axis=0, keepdims=True)
    held = jnp.sum((rows_down == lane).astype(jnp.int32), axis=0, keepdims=True)
    order_vmem[1:2] = jnp.where(held > 0, upto - 1, KT)
    ordering = pltpu.make_async_copy(order_vmem, order, order_sem)
    ordering.start()

    def share(c, par, g):
        mine = land.at[c, par, pl.ds(gy * RB + g * G, G)]
        for d in (2, 1, 3):
            remote(mine, mine, share_send.at[c, par, d - 1], share_recv.at[c, par, d - 1], at_gy(d)).start()

    def gathered(c, par):
        four = land.at[c, par, pl.ds(0, RB)]
        for sem in (share_recv, share_send):
            for d in (1, 2, 3):
                wait_for(four, sem.at[c, par, d - 1])

    def row_of(h, b, d1, d2):
        dy, dz = (d1, d2) if h == 0 else (d2, d1)
        return order[1, ((y + dy) % 4 * 4 + (zc + dz) % 4) * RB + b]

    def partial(h, b, d1, d2):
        return s[row_of(h, b, d1, d2), h * HP:(h + 1) * HP]

    def fill(c, h, g, m):
        at, n = FIRST[m]
        for i in range(at, at + n):
            for k in range(G):
                p[c, h, g, i, k] = partial(h, g * G + k, *CHUNKS[i])

    def send1(c, par, h, g, m):
        at, n = FIRST[m]
        remote(p.at[c, h, g, pl.ds(at, n)], r1.at[c, par, h, g, pl.ds(at, n)], psend.at[c],
               rs1.at[c, par, h, g, m], first_axis[h](1 if m % 2 == 0 else 3)).start()

    def arrived1(c, par, h, g, m):
        at, n = FIRST[m]
        wait_for(r1.at[c, par, h, g, pl.ds(at, n)], rs1.at[c, par, h, g, m])

    def begin(c, par):
        for pair in ((0, 1), (2, 3)):
            for g in range(PC):
                for h in (0, 1):
                    for m in pair:
                        fill(c, h, g, m)
                        send1(c, par, h, g, m)
        for g in range(PC):
            for h in (0, 1):
                for m in (4, 5):
                    fill(c, h, g, m)
                for d in range(4):
                    for k in range(G):
                        own[c, h, g, d, k] = partial(h, g * G + k, 0, d)

    def hand_on(c, par, g):
        for h in (0, 1):
            for m in (0, 1):
                arrived1(c, par, h, g, m)
                to, came = FIRST[m + 4][0], FIRST[m][0]
                for i in range(2):
                    p[c, h, g, to + i] = (p[c, h, g, to + i].astype(F32)
                                          + r1[c, par, h, g, came + i].astype(F32)).astype(BF16)
                send1(c, par, h, g, m + 4)

    def scale(a):
        return jnp.where(a == 0, 1.0, 2.0).astype(F32)

    def second(c, a, par, g):
        for h in (0, 1):
            form = jnp.zeros((HP, BS), F32)
            for m in (2, 3, 4, 5):
                arrived1(c, par, h, g, m)
            for d in (2, 1, 3, 0):
                up, down = (4 + d, 8 + d) if d < 2 else (d, 8 + d)
                for k in range(G):
                    total = (own[c, h, g, d, k].astype(F32)
                             + r1[c, par, h, g, up, k].astype(F32) + r1[c, par, h, g, down, k].astype(F32))
                    b = g * G + k
                    if d:
                        q[c, h, g, d - 1, k] = total.astype(BF16)
                        form = form + zg[c, h, d - 1, b].astype(F32) * (scale(a) * total)
                    else:
                        qown[c, h, g, k] = total
                        form = form + z[c, h, b] * (scale(a) * (total + shift[:, b * BS:(b + 1) * BS] * t[par, c, h, b])
                                                    - t[1 - par, c, h, b])
                if d:
                    remote(q.at[c, h, g, d - 1], r2.at[c, par, h, g, d - 1], qsend.at[c],
                           rs2.at[c, par, h, g, d - 1], second_axis[h](d)).start()
            fsum[a, c, h] += form[:, :NP] + form[:, NP:]

    def finish(c, a, par, g):
        nxt = 1 - par
        for h in (0, 1):
            for d in (0, 1, 2):
                wait_for(r2.at[c, par, h, g, d], rs2.at[c, par, h, g, d])
            for k in range(G):
                b = g * G + k
                m_w = qown[c, h, g, k]
                for d in (0, 1, 2):
                    m_w = m_w + r2[c, par, h, g, d, k].astype(F32)
                new = scale(a) * (m_w + shift[:, b * BS:(b + 1) * BS] * t[par, c, h, b]) - t[nxt, c, h, b]
                t[nxt, c, h, b] = new
                land[c, nxt, gy * RB + b, h * HP:(h + 1) * HP] = new.astype(BF16)

        @pl.when(a < 2)
        def _():
            share(c, nxt, g)

    def sent(c):
        wait_for(p.at[c], psend.at[c])
        wait_for(q.at[c], qsend.at[c])

    pl.semaphore_wait(barrier, 9)
    for c in range(NC):
        for g in range(PC):
            share(c, 0, g)
    for d in (1, 3, 2):
        for c in range(NC):
            for h in (0, 1):
                remote(zb.at[c, h], zg.at[c, h, 3 - d], zsend, zrecv, second_axis[h](d)).start()
    ordering.wait()

    def turn(i, _):
        load(i).wait()
        for u in range(LOAD):
            blocks[i * LOAD + u] = blocks[i * LOAD + u].T
        return 0

    lax.fori_loop(0, KT // LOAD, turn, 0)

    def block(k, carry):
        acc, prev = carry
        e = order[0, k]
        row = e >> 11
        keep = (row == prev).astype(F32)
        acc = acc * keep + jnp.dot(w[(e >> 7) & 15], blocks[e & 127], preferred_element_type=F32)
        s[k] = acc.astype(BF16)
        return acc, row

    def group(i, carry):
        for u in range(UNROLL):
            carry = block(i * UNROLL + u, carry)
        return carry

    def take(c, par):
        gathered(c, par)
        w[...] = land[c, par]

    steps = {
        "w": lambda c, a, par, g: take(c, par),
        "b": lambda c, a, par, g: begin(c, par),
        "h": lambda c, a, par, g: hand_on(c, par, g),
        "s": second,
        "f": finish,
        "e": lambda c, a, par, g: sent(c),
    }

    def do(token, n):
        step, lag = token.split(".")
        m = n - int(lag)
        steps[step[0]](m % NC, m // NC, m // NC % 2, int(step[1:] or 0))

    def phase(n, _):
        @pl.when(n == 1)
        def _():
            wait_for(zg, zrecv)
            wait_for(zg, zsend)

        carry = (jnp.zeros((CP, BS), F32), jnp.int32(-1))
        for token in ORDER:
            lag = int(token.split(".")[1])
            if token[0] == "m":
                carry = group(int(token[1:-2]), carry)
            elif lag == 0:
                do(token, n)
            else:
                @pl.when(n >= lag)
                def _():
                    do(token, n)
        return 0

    phases = 3 * NC
    lax.fori_loop(0, phases, phase, 0)

    def exchange(stage):
        there = (at_gy, at_y, at_z)[stage]
        return [remote(fs.at[stage], fr.at[stage, d - 1], fsend.at[stage, d - 1], frecv.at[stage, d - 1], there(d))
                for d in (2, 1, 3)]

    def total_of(stage):
        for copy in exchange(stage):
            copy.wait()
        return fs[stage] + fr[stage, 0] + fr[stage, 1] + fr[stage, 2]

    def go(stage):
        for copy in exchange(stage):
            copy.start()

    final = NC - 1
    for g in range(PC):
        second(final, 2, 0, g)
    fs[0] = jnp.zeros((8, NP), F32)
    for k in range(3):
        fs[0, k:k + 1] = jnp.sum(fsum[k].reshape(NP, NP).T, axis=0, keepdims=True)
    go(0)
    finish(final, 2, 0, 0)
    finish(final, 2, 0, 1)
    fs[1] = total_of(0)
    go(1)
    for g in range(2, PC):
        finish(final, 2, 0, g)
    for r in range(LOC // NP):
        part_rows = t[1, :, :, r // 2, :, r % 2 * NP:r % 2 * NP + NP].reshape(NP, NP)
        out[r * NP:(r + 1) * NP] = part_rows.T
    result = pltpu.make_async_copy(out, out_hbm, out_sem)
    result.start()
    sent(final)
    fs[2] = total_of(1)
    go(2)
    forms[...] = total_of(2)[:3]
    result.wait()


def body(blocks, block_rows, block_cols, probe_bits, shift):
    dma = pltpu.SemaphoreType.DMA
    out, forms = pl.pallas_call(
        kernel,
        out_shape=(
            jax.ShapeDtypeStruct((LOC, NP), F32),
            jax.ShapeDtypeStruct((3, NP), F32),
        ),
        in_specs=[
            pl.BlockSpec(memory_space=pltpu.VMEM),
            pl.BlockSpec(memory_space=pltpu.VMEM),
            pl.BlockSpec(memory_space=pl.ANY),
            pl.BlockSpec(memory_space=pltpu.VMEM),
            pl.BlockSpec(memory_space=pltpu.VMEM),
        ],
        out_specs=(
            pl.BlockSpec(memory_space=pl.ANY),
            pl.BlockSpec(memory_space=pltpu.VMEM),
        ),
        scratch_shapes=[
            pltpu.VMEM((KT, BS, BS), BF16),
            pltpu.VMEM((KT + 1, CP, BS), BF16),
            pltpu.VMEM((TC, CP, BS), BF16),
            pltpu.VMEM((NC, 2, TC, CP, BS), BF16),
            pltpu.VMEM((2, NC, 2, RB, HP, BS), F32),
            pltpu.VMEM((NC, 2, RB, HP, BS), F32),
            pltpu.VMEM((NC, 2, RB, HP, BS), BF16),
            pltpu.VMEM((NC, 2, 3, RB, HP, BS), BF16),
            pltpu.VMEM((NC, 2, PC, 12, G, HP, BS), BF16),
            pltpu.VMEM((NC, 2, PC, 4, G, HP, BS), BF16),
            pltpu.VMEM((NC, 2, 2, PC, 12, G, HP, BS), BF16),
            pltpu.VMEM((NC, 2, PC, 3, G, HP, BS), BF16),
            pltpu.VMEM((NC, 2, PC, G, HP, BS), F32),
            pltpu.VMEM((NC, 2, 2, PC, 3, G, HP, BS), BF16),
            pltpu.VMEM((3, NC, 2, HP, NP), F32),
            pltpu.VMEM((3, 8, NP), F32),
            pltpu.VMEM((3, 3, 8, NP), F32),
            pltpu.VMEM((LOC, NP), F32),
            pltpu.VMEM((8, KT), jnp.int32),
            pltpu.SMEM((8, KT), jnp.int32),
            dma((KT // LOAD,)), dma, dma,
            dma((NC,)), dma((NC,)),
            dma, dma,
            dma((NC, 2, 2, PC, 6)),
            dma((NC, 2, 2, PC, 3)),
            dma((NC, 2, 3)), dma((NC, 2, 3)),
            dma((3, 3)), dma((3, 3)),
        ],
        compiler_params=pltpu.CompilerParams(
            collective_id=0, has_side_effects=True, vmem_limit_bytes=60 * 2**20
        ),
        cost_estimate=pl.CostEstimate(
            flops=6 * KT * BS * BS * NP, bytes_accessed=18 * 2**20, transcendentals=0
        ),
    )(block_rows[0], block_cols[0], blocks[0, 0], probe_bits, shift[None])
    return forms, out


def solution(mesh):
    return jax.shard_map(
        body,
        mesh=mesh,
        in_specs=(
            P("gy", "gx", None, None, None),
            P("gy", "gx", None),
            P("gy", "gx", None),
            P(("gy", "gx"), "gz"),
            P(("gy", "gx")),
        ),
        out_specs=(P(None, "gz"), P(("gy", "gx"), "gz")),
        check_vma=False,
    )
```

```python
import jax
import jax.numpy as jnp
from jax import lax
from jax.experimental import pallas as pl
from jax.experimental.pallas import tpu as pltpu
from jax.sharding import PartitionSpec as P

BS = 256
KT = 128
TR = 64
TC = 16
NP = 128
NC = 2
CP = NP // NC
HP = CP // 2
RB = 4
PC = 4
G = RB // PC
LOC = RB * BS
F32 = jnp.float32
BF16 = jnp.bfloat16
UNROLL = 32
LATER = 2
LOAD = 16
ORDER = ('w.0', 'm0.0', 's0.1', 'm1.0', 's1.1', 'm2.0', 's2.1', 'm3.0', 's3.1', 'b.0', 'f0.1', 'f1.1', 'f2.1', 'f3.1', 'e.1', 'h0.0', 'h1.0', 'h2.0', 'h3.0')


CHUNKS = ((2, 0), (2, 1), (1, 2), (1, 3), (1, 0), (1, 1),
          (2, 2), (2, 3), (3, 0), (3, 1), (3, 2), (3, 3))
FIRST = ((0, 2), (6, 2), (2, 2), (8, 2), (4, 2), (10, 2))


def kernel(rows, cols, blocks_hbm, bits, shift, out_hbm, forms,
           blocks, s, w, land, t, z, zb, zg, p, own, r1, q, qown, r2, fsum, fs, fr, out,
           order_vmem, order, load_sem, order_sem, out_sem, psend, qsend, zsend, zrecv, rs1, rs2, share_send, share_recv,
           fsend, frecv):
    gx, gy, gz = lax.axis_index("gx"), lax.axis_index("gy"), lax.axis_index("gz")
    y, zc = gx // 4, gx % 4
    def at_y(d):
        return {"gx": (y + d) % 4 * 4 + zc, "gy": gy, "gz": gz}

    def at_z(d):
        return {"gx": y * 4 + (zc + d) % 4, "gy": gy, "gz": gz}

    def at_gy(d):
        other_core = gy + 1 - 2 * (gy % 2)
        return {"gx": gx, "gy": ((gy if d == 2 else other_core) + (2 if d > 1 else 0)) % 4, "gz": gz}

    first_axis, second_axis = (at_y, at_z), (at_z, at_y)

    def load(i):
        part = pl.ds(i * LOAD, LOAD)
        return pltpu.make_async_copy(blocks_hbm.at[part], blocks.at[part], load_sem.at[i])

    for i in range(KT // LOAD):
        load(i).start()

    barrier = pltpu.get_barrier_semaphore()
    for d in (1, 2, 3):
        for there in (at_y, at_z, at_gy):
            pl.semaphore_signal(barrier, inc=1, device_id=there(d), device_id_type=pl.DeviceIdType.MESH)

    def remote(src, dst, send, recv, where):
        return pltpu.make_async_remote_copy(
            src_ref=src, dst_ref=dst, send_sem=send, recv_sem=recv,
            device_id=where, device_id_type=pl.DeviceIdType.MESH)

    def wait_for(ref, sem):
        pltpu.make_async_copy(ref, ref, sem).wait()

    for r in range(LOC // NP):
        signs = (2 * bits[r * NP:(r + 1) * NP] - 1).astype(F32).T
        b, lanes = r // 2, slice(r % 2 * NP, r % 2 * NP + NP)
        for c in range(NC):
            for h in (0, 1):
                mine = signs[(2 * c + h) * HP:(2 * c + h + 1) * HP]
                z[c, h, b, :, lanes] = mine
                zb[c, h, b, :, lanes] = mine.astype(BF16)
                t[0, c, h, b, :, lanes] = mine
                land[c, 0, gy * RB + b, h * HP:(h + 1) * HP, lanes] = mine.astype(BF16)
    t[1] = jnp.zeros_like(t[1])
    fsum[...] = jnp.zeros_like(fsum)
    s[KT] = jnp.zeros((CP, BS), BF16)

    lane = lax.broadcasted_iota(jnp.int32, (KT, KT), 1)
    stored = lax.broadcasted_iota(jnp.int32, (KT, KT), 0)
    rows_across = jnp.broadcast_to(rows[...], (KT, KT))
    rows_down = rows_across.astype(F32).T.astype(jnp.int32)
    cols_down = jnp.broadcast_to(cols[...], (KT, KT)).astype(F32).T.astype(jnp.int32)
    before = rows_across * KT + lane < rows_down * KT + stored
    rank = jnp.sum(before.astype(jnp.int32), axis=1, keepdims=True)
    entry = (rows_down * TC + cols_down) * KT + stored
    order_vmem[...] = jnp.zeros_like(order_vmem)
    order_vmem[0:1] = jnp.sum(jnp.where(rank == lane, entry, 0), axis=0, keepdims=True)
    upto = jnp.sum((rows_down <= lane).astype(jnp.int32), axis=0, keepdims=True)
    held = jnp.sum((rows_down == lane).astype(jnp.int32), axis=0, keepdims=True)
    order_vmem[1:2] = jnp.where(held > 0, upto - 1, KT)
    ordering = pltpu.make_async_copy(order_vmem, order, order_sem)
    ordering.start()

    def share(c, par, g):
        mine = land.at[c, par, pl.ds(gy * RB + g * G, G)]
        for d in (2, 1, 3):
            remote(mine, mine, share_send.at[c, par, d - 1], share_recv.at[c, par, d - 1], at_gy(d)).start()

    def gathered(c, par):
        four = land.at[c, par, pl.ds(0, RB)]
        for sem in (share_recv, share_send):
            for d in (1, 2, 3):
                wait_for(four, sem.at[c, par, d - 1])

    def row_of(h, b, d1, d2):
        dy, dz = (d1, d2) if h == 0 else (d2, d1)
        return order[1, ((y + dy) % 4 * 4 + (zc + dz) % 4) * RB + b]

    def partial(h, b, d1, d2):
        return s[row_of(h, b, d1, d2), h * HP:(h + 1) * HP]

    def fill(c, h, g, m):
        at, n = FIRST[m]
        for i in range(at, at + n):
            for k in range(G):
                p[c, h, g, i, k] = partial(h, g * G + k, *CHUNKS[i])

    def send1(c, par, h, g, m):
        at, n = FIRST[m]
        remote(p.at[c, h, g, pl.ds(at, n)], r1.at[c, par, h, g, pl.ds(at, n)], psend.at[c],
               rs1.at[c, par, h, g, m], first_axis[h](1 if m % 2 == 0 else 3)).start()

    def arrived1(c, par, h, g, m):
        at, n = FIRST[m]
        wait_for(r1.at[c, par, h, g, pl.ds(at, n)], rs1.at[c, par, h, g, m])

    def begin(c, par):
        for pair in ((0, 1), (2, 3)):
            for g in range(PC):
                for h in (0, 1):
                    for m in pair:
                        fill(c, h, g, m)
                        if m < 2 or g < PC - LATER:
                            send1(c, par, h, g, m)
        for g in range(PC):
            for h in (0, 1):
                for m in (4, 5):
                    fill(c, h, g, m)
                for d in range(4):
                    for k in range(G):
                        own[c, h, g, d, k] = partial(h, g * G + k, 0, d)

    def hand_on(c, par, g):
        for h in (0, 1):
            for m in (0, 1):
                arrived1(c, par, h, g, m)
                to, came = FIRST[m + 4][0], FIRST[m][0]
                for i in range(2):
                    p[c, h, g, to + i] = (p[c, h, g, to + i].astype(F32)
                                          + r1[c, par, h, g, came + i].astype(F32)).astype(BF16)
                send1(c, par, h, g, m + 4)
                if g < LATER:
                    send1(c, par, h, g + PC - LATER, m + 2)

    def scale(a):
        return jnp.where(a == 0, 1.0, 2.0).astype(F32)

    def second(c, a, par, g):
        for h in (0, 1):
            form = jnp.zeros((HP, BS), F32)
            for m in (2, 3, 4, 5):
                arrived1(c, par, h, g, m)
            for d in (2, 1, 3, 0):
                up, down = (4 + d, 8 + d) if d < 2 else (d, 8 + d)
                for k in range(G):
                    total = (own[c, h, g, d, k].astype(F32)
                             + r1[c, par, h, g, up, k].astype(F32) + r1[c, par, h, g, down, k].astype(F32))
                    b = g * G + k
                    if d:
                        q[c, h, g, d - 1, k] = total.astype(BF16)
                        form = form + zg[c, h, d - 1, b].astype(F32) * (scale(a) * total)
                    else:
                        qown[c, h, g, k] = total
                        form = form + z[c, h, b] * (scale(a) * (total + shift[:, b * BS:(b + 1) * BS] * t[par, c, h, b])
                                                    - t[1 - par, c, h, b])
                if d:
                    remote(q.at[c, h, g, d - 1], r2.at[c, par, h, g, d - 1], qsend.at[c],
                           rs2.at[c, par, h, g, d - 1], second_axis[h](d)).start()
            fsum[a, c, h] += form[:, :NP] + form[:, NP:]

    def finish(c, a, par, g):
        nxt = 1 - par
        for h in (0, 1):
            for d in (0, 1, 2):
                wait_for(r2.at[c, par, h, g, d], rs2.at[c, par, h, g, d])
            for k in range(G):
                b = g * G + k
                m_w = qown[c, h, g, k]
                for d in (0, 1, 2):
                    m_w = m_w + r2[c, par, h, g, d, k].astype(F32)
                new = scale(a) * (m_w + shift[:, b * BS:(b + 1) * BS] * t[par, c, h, b]) - t[nxt, c, h, b]
                t[nxt, c, h, b] = new
                land[c, nxt, gy * RB + b, h * HP:(h + 1) * HP] = new.astype(BF16)

        @pl.when(a < 2)
        def _():
            share(c, nxt, g)

    def sent(c):
        wait_for(p.at[c], psend.at[c])
        wait_for(q.at[c], qsend.at[c])

    pl.semaphore_wait(barrier, 9)
    for c in range(NC):
        for g in range(PC):
            share(c, 0, g)
    for d in (1, 3, 2):
        for c in range(NC):
            for h in (0, 1):
                remote(zb.at[c, h], zg.at[c, h, 3 - d], zsend, zrecv, second_axis[h](d)).start()
    ordering.wait()

    def turn(i, _):
        load(i).wait()
        for u in range(LOAD):
            blocks[i * LOAD + u] = blocks[i * LOAD + u].T
        return 0

    lax.fori_loop(0, KT // LOAD, turn, 0)

    def block(k, carry):
        acc, prev = carry
        e = order[0, k]
        row = e >> 11
        keep = (row == prev).astype(F32)
        acc = acc * keep + jnp.dot(w[(e >> 7) & 15], blocks[e & 127], preferred_element_type=F32)
        s[k] = acc.astype(BF16)
        return acc, row

    def group(i, carry):
        for u in range(UNROLL):
            carry = block(i * UNROLL + u, carry)
        return carry

    def take(c, par):
        gathered(c, par)
        w[...] = land[c, par]

    steps = {
        "w": lambda c, a, par, g: take(c, par),
        "b": lambda c, a, par, g: begin(c, par),
        "h": lambda c, a, par, g: hand_on(c, par, g),
        "s": second,
        "f": finish,
        "e": lambda c, a, par, g: sent(c),
    }

    def do(token, n):
        step, lag = token.split(".")
        m = n - int(lag)
        steps[step[0]](m % NC, m // NC, m // NC % 2, int(step[1:] or 0))

    def phase(n, _):
        @pl.when(n == 1)
        def _():
            wait_for(zg, zrecv)
            wait_for(zg, zsend)

        carry = (jnp.zeros((CP, BS), F32), jnp.int32(-1))
        for token in ORDER:
            lag = int(token.split(".")[1])
            if token[0] == "m":
                carry = group(int(token[1:-2]), carry)
            elif lag == 0:
                do(token, n)
            else:
                @pl.when(n >= lag)
                def _():
                    do(token, n)
        return 0

    phases = 3 * NC
    lax.fori_loop(0, phases, phase, 0)

    def exchange(stage):
        there = (at_gy, at_y, at_z)[stage]
        return [remote(fs.at[stage], fr.at[stage, d - 1], fsend.at[stage, d - 1], frecv.at[stage, d - 1], there(d))
                for d in (2, 1, 3)]

    def total_of(stage):
        for copy in exchange(stage):
            copy.wait()
        return fs[stage] + fr[stage, 0] + fr[stage, 1] + fr[stage, 2]

    def go(stage):
        for copy in exchange(stage):
            copy.start()

    final = NC - 1
    for g in range(PC):
        second(final, 2, 0, g)
    fs[0] = jnp.zeros((8, NP), F32)
    for k in range(3):
        fs[0, k:k + 1] = jnp.sum(fsum[k].reshape(NP, NP).T, axis=0, keepdims=True)
    go(0)
    finish(final, 2, 0, 0)
    finish(final, 2, 0, 1)
    fs[1] = total_of(0)
    go(1)
    for g in range(2, PC):
        finish(final, 2, 0, g)
    for r in range(LOC // NP):
        part_rows = t[1, :, :, r // 2, :, r % 2 * NP:r % 2 * NP + NP].reshape(NP, NP)
        out[r * NP:(r + 1) * NP] = part_rows.T
    result = pltpu.make_async_copy(out, out_hbm, out_sem)
    result.start()
    sent(final)
    fs[2] = total_of(1)
    go(2)
    forms[...] = total_of(2)[:3]
    result.wait()


def body(blocks, block_rows, block_cols, probe_bits, shift):
    dma = pltpu.SemaphoreType.DMA
    out, forms = pl.pallas_call(
        kernel,
        out_shape=(
            jax.ShapeDtypeStruct((LOC, NP), F32),
            jax.ShapeDtypeStruct((3, NP), F32),
        ),
        in_specs=[
            pl.BlockSpec(memory_space=pltpu.VMEM),
            pl.BlockSpec(memory_space=pltpu.VMEM),
            pl.BlockSpec(memory_space=pl.ANY),
            pl.BlockSpec(memory_space=pltpu.VMEM),
            pl.BlockSpec(memory_space=pltpu.VMEM),
        ],
        out_specs=(
            pl.BlockSpec(memory_space=pl.ANY),
            pl.BlockSpec(memory_space=pltpu.VMEM),
        ),
        scratch_shapes=[
            pltpu.VMEM((KT, BS, BS), BF16),
            pltpu.VMEM((KT + 1, CP, BS), BF16),
            pltpu.VMEM((TC, CP, BS), BF16),
            pltpu.VMEM((NC, 2, TC, CP, BS), BF16),
            pltpu.VMEM((2, NC, 2, RB, HP, BS), F32),
            pltpu.VMEM((NC, 2, RB, HP, BS), F32),
            pltpu.VMEM((NC, 2, RB, HP, BS), BF16),
            pltpu.VMEM((NC, 2, 3, RB, HP, BS), BF16),
            pltpu.VMEM((NC, 2, PC, 12, G, HP, BS), BF16),
            pltpu.VMEM((NC, 2, PC, 4, G, HP, BS), BF16),
            pltpu.VMEM((NC, 2, 2, PC, 12, G, HP, BS), BF16),
            pltpu.VMEM((NC, 2, PC, 3, G, HP, BS), BF16),
            pltpu.VMEM((NC, 2, PC, G, HP, BS), F32),
            pltpu.VMEM((NC, 2, 2, PC, 3, G, HP, BS), BF16),
            pltpu.VMEM((3, NC, 2, HP, NP), F32),
            pltpu.VMEM((3, 8, NP), F32),
            pltpu.VMEM((3, 3, 8, NP), F32),
            pltpu.VMEM((LOC, NP), F32),
            pltpu.VMEM((8, KT), jnp.int32),
            pltpu.SMEM((8, KT), jnp.int32),
            dma((KT // LOAD,)), dma, dma,
            dma((NC,)), dma((NC,)),
            dma, dma,
            dma((NC, 2, 2, PC, 6)),
            dma((NC, 2, 2, PC, 3)),
            dma((NC, 2, 3)), dma((NC, 2, 3)),
            dma((3, 3)), dma((3, 3)),
        ],
        compiler_params=pltpu.CompilerParams(
            collective_id=0, has_side_effects=True, vmem_limit_bytes=60 * 2**20
        ),
        cost_estimate=pl.CostEstimate(
            flops=6 * KT * BS * BS * NP, bytes_accessed=18 * 2**20, transcendentals=0
        ),
    )(block_rows[0], block_cols[0], blocks[0, 0], probe_bits, shift[None])
    return forms, out


def solution(mesh):
    return jax.shard_map(
        body,
        mesh=mesh,
        in_specs=(
            P("gy", "gx", None, None, None),
            P("gy", "gx", None),
            P("gy", "gx", None),
            P(("gy", "gx"), "gz"),
            P(("gy", "gx")),
        ),
        out_specs=(P(None, "gz"), P(("gy", "gx"), "gz")),
        check_vma=False,
    )
```
